768 devices in a mesh: comp: 8 (over y), dom: 96 (over z, x, core).
Axes of the slice: x: 4, y: 8, z: 12, core: 2. Of those that a mesh axis runs over, the one named last changes fastest.
Arguments:
- atm_fields: bfloat16 [24, 1572864], P(None, ('comp', 'dom')), may hold values from -6 to 6
- send_cols: int32 [8, 96, 8, 4, 256], P('comp', 'dom'), may hold values from 0 to 2047
- live_blocks: int32 [8, 96, 8], P('comp', 'dom'), may hold values from 1 to 4, as said below
- remap_weights: bfloat16 [8, 96, 8, 4, 256, 256], P('comp', 'dom'), may hold values from -0.375 to 0.375
- row_map: int32 [8, 96, 8, 4, 256], P('comp', 'dom'), may hold values from 0 to 4095
- ocean_depth: float32 [3072, 1024], P('dom', 'comp'), may hold values from 0.25 to 8
- wet_mask: int32 [3072, 1024], P('dom', 'comp'), may hold values 0 or 1
- sea_level: float32 [3072, 1024], P('dom', 'comp'), may hold values from -3 to 3
- east_vel: float32 [3072, 1024], P('dom', 'comp'), may hold values from -0.3 to 0.3
- north_vel: float32 [3072, 1024], P('dom', 'comp'), may hold values from -0.3 to 0.3
Outputs:
- ocean_fluxes: float32 [24, 3072, 1024], P(None, 'dom', 'comp')
- ocean_state: float32 [3, 3072, 1024], P(None, 'dom', 'comp')
The draws below stay inside these ranges and needn't reach their ends.
Inputs may be any that keep to these rules, and one draw needn't show every extreme that they name: `live_blocks`: every receiving device has exactly 4 live blocks from at least one source group.
All inputs are finite; a program needn't handle non-finite values. No bound on the sum of `wet_mask` on one device may be relied on, other than what follows from the above.
Results may differ from the reference program's by a relative error of at most 0.0003.
Values may be sent and summed in bfloat16 or wider, within the bound.
No kernel may reach another device: no remote copies, remote signals or barrier semaphores. Data moves between devices by JAX's collectives and lax.ppermute only.
A program may use at most 64 MiB of HBM per device.

```python
import jax
import jax.numpy as jnp
from jax import lax

F = 24
AC = 2048
AB = 256
OB = 256
CAP = 4
RO = 32
CO = 128
NSUB = 4
NAC = 1572864
NR = 3072
NCOL = 1024
N_COMP = 8
N_DOM = 96


def draw_ocean_depth(key, part):
    rows_frac = jnp.arange(NR, dtype=jnp.float32)[:, None] / NR
    cols_frac = jnp.arange(NCOL, dtype=jnp.float32)[None, :] / NCOL
    trend = 0.5 * jnp.power(16.0, 0.5 * (rows_frac + cols_frac))
    rough = jnp.exp(jax.random.uniform(key, (NR, NCOL), jnp.float32, -0.69, 0.0))
    return jnp.clip(trend * rough, 0.25, 8.0)


def draw_live_blocks(key, part):
    first = jax.random.fold_in(key, 11)
    second = jax.random.fold_in(key, 23)
    base = jax.random.randint(first, (N_COMP, N_DOM, N_COMP), 1, CAP + 1)
    chosen = jax.random.randint(second, (N_COMP, N_DOM, 1), 0, N_COMP)
    source = jnp.arange(N_COMP, dtype=jnp.int32)[None, None, :]
    return jnp.where(source == chosen, CAP, base).astype(jnp.int32)


def touch_ends(array, stream_key, least, top_value):
    dims = array.shape
    place = [jax.random.randint(jax.random.fold_in(stream_key, axis), (), 0, dims[axis]) for axis in range(len(dims))]
    array = array.at[tuple(place)].set(least)
    longest = dims.index(max(dims))
    place[longest] = (place[longest] + 1) % dims[longest]
    return array.at[tuple(place)].set(top_value)


def block_levels(key, dims, split, smallest, top_value):
    def one(axis_at, parts):
        heights = jax.random.uniform(jax.random.fold_in(jax.random.fold_in(key, 6), axis_at), (parts,), jnp.float32, smallest / len(split), top_value / len(split))
        return jnp.repeat(jnp.exp(heights), dims[axis_at] // parts).reshape((-1,) + (1,) * (len(dims) - axis_at - 1))

    factor_of = one(*split[0])
    for cut in split[1:]:
        factor_of = factor_of * one(*cut)
    return factor_of


def gaussian(rng, shape, spread, reach, shards=(), held_as=jnp.bfloat16):
    values = spread * jax.random.normal(rng, shape, jnp.float32)
    if shards:
        values = values * block_levels(rng, shape, shards, -0.22, 0.18)
    return jnp.clip(values, -reach, reach).astype(held_as)


def setup_inputs(seed: int = 0) -> dict:
    streams_of = jax.random.split(jax.random.key(seed), 11)
    return {
        "atm_fields": gaussian(streams_of[0], (F, NAC), 1.0, 6.0, ((1, 768),)),
        "send_cols": touch_ends(jax.random.randint(streams_of[1], (N_COMP, N_DOM, N_COMP, CAP, AB), 0, AC), jax.random.fold_in(streams_of[1], 1), 0, AC - 1).astype(jnp.int32),
        "live_blocks": draw_live_blocks(jax.random.fold_in(streams_of[10], 71), 0),
        "remap_weights": gaussian(streams_of[3], (N_COMP, N_DOM, N_COMP, CAP, OB, AB), AB ** -0.5, 0.375, ((0, 8), (1, 96))),
        "row_map": touch_ends(jax.random.randint(streams_of[4], (N_COMP, N_DOM, N_COMP, CAP, OB), 0, RO * CO), jax.random.fold_in(streams_of[4], 1), 0, (RO * CO) - 1).astype(jnp.int32),
        "ocean_depth": draw_ocean_depth(jax.random.fold_in(streams_of[10], 71), 0),
        "wet_mask": touch_ends((jax.random.randint(streams_of[6], (NR, NCOL), 0, 10) < 9).astype(jnp.int32), jax.random.fold_in(streams_of[6], 1), 0, 1),
        "sea_level": gaussian(streams_of[7], (NR, NCOL), 0.5, 3.0, ((0, 96), (1, 8)), jnp.float32),
        "east_vel": gaussian(streams_of[8], (NR, NCOL), 0.1, 0.3, ((0, 96), (1, 8)), jnp.float32),
        "north_vel": gaussian(streams_of[9], (NR, NCOL), 0.1, 0.3, ((0, 96), (1, 8)), jnp.float32),
    }


courant = 0.5
friction = 0.05

def level_update(level, flux_x, flux_y, fresh, wetness, step_dt):
    diverge = 0.5 * (flux_x[1:-1, 2:] - flux_x[1:-1, :-2] + (flux_y[2:, 1:-1] - flux_y[:-2, 1:-1]))
    return wetness[1:-1, 1:-1] * (level[1:-1, 1:-1] + step_dt * (fresh[1:-1, 1:-1] - diverge))

def velocity_update(east, north, level_ext, rotation, push_x, push_y, wetness, step_dt):
    grad_x = 0.5 * (level_ext[1:-1, 2:] - level_ext[1:-1, :-2])
    grad_y = 0.5 * (level_ext[2:, 1:-1] - level_ext[:-2, 1:-1])
    new_east = wetness * (east + step_dt * (rotation * north - grad_x + push_x - friction * east))
    new_north = wetness * (north + step_dt * (-rotation * east - grad_y + push_y - friction * north))
    return (new_east, new_north)

def reference(atm_fields, send_cols, live_blocks, remap_weights, row_map, ocean_depth, wet_mask, sea_level, east_vel, north_vel):
    fields = atm_fields.reshape(F, N_COMP, N_DOM, AC)
    slots = jnp.arange(CAP, dtype=jnp.int32)

    def one_device(index):
        group = index // N_DOM
        part_d = index % N_DOM
        cols = send_cols[:, part_d, group]
        sources = jnp.transpose(fields[:, :, part_d, :], (1, 0, 2))
        blocks = jax.vmap(lambda source, column: jnp.take(source, column.reshape(-1), axis=1).reshape(F, CAP, AB))(sources, cols)
        weights = remap_weights[group, part_d]
        contrib = jnp.einsum('sfkb,skob->skfo', blocks.astype(jnp.float32), weights.astype(jnp.float32))
        alive = (slots[None, :] < live_blocks[group, part_d][:, None]).astype(jnp.float32)
        contrib = contrib * alive[:, :, None, None]
        flat = jnp.transpose(contrib, (2, 0, 1, 3)).reshape(F, -1)
        total = jnp.zeros((F, RO * CO), jnp.float32).at[:, row_map[group, part_d].reshape(-1)].add(flat)
        return total.reshape(F, RO, CO)
    blocks_out = lax.map(one_device, jnp.arange(N_COMP * N_DOM, dtype=jnp.int32))
    fluxes = blocks_out.reshape(N_COMP, N_DOM, F, RO, CO)
    fluxes = jnp.transpose(fluxes, (2, 1, 3, 0, 4)).reshape(F, NR, NCOL)
    wetness = wet_mask.astype(jnp.float32)
    push_x = fluxes[0] / ocean_depth
    push_y = fluxes[1] / ocean_depth
    fresh = fluxes[2]
    rows_idx = jnp.arange(NR, dtype=jnp.float32)
    rotation = (0.1 + 0.4 * (rows_idx + 0.5) / NR)[:, None]

    def padded(value):
        return jnp.pad(value, 1)
    level, east, north = (sea_level, east_vel, north_vel)
    for substep in range(NSUB):
        speed = jnp.sqrt(ocean_depth) + wetness * (jnp.abs(east) + jnp.abs(north))
        step_dt = courant / jnp.max(speed)
        flux_x = ocean_depth * east * wetness
        flux_y = ocean_depth * north * wetness
        new_level = level_update(padded(level), padded(flux_x), padded(flux_y), padded(fresh), padded(wetness), step_dt)
        east, north = velocity_update(east, north, padded(new_level), rotation, push_x, push_y, wetness, step_dt)
        level = new_level
    return (fluxes, jnp.stack([level, east, north]))
```

```python
import functools

import jax
import jax.numpy as jnp
from jax import lax
from jax.experimental import pallas as pl
from jax.experimental.pallas import tpu as pltpu
from jax.sharding import Mesh
from jax.sharding import PartitionSpec as P

NSUB = 4
DOM_SHAPE = (12, 4, 2)
COMP_DOM = ("comp", "dom_0", "dom_1", "dom_2")
DOM = ("dom_0", "dom_1", "dom_2")
PLANE = ("comp", "dom_1")
COLUMN = ("dom_0", "dom_2")
BF16 = jnp.bfloat16
F32 = jnp.float32

courant = 0.5
friction = 0.05

EDGE = 8


def params(mib=48, **kwargs):
    return pltpu.CompilerParams(vmem_limit_bytes=mib * 1024 * 1024, **kwargs)


def axes_size(axes):
    return functools.reduce(lambda a, b: a * b, [lax.axis_size(a) for a in axes])


def neighbours(array, axes):
    count = axes_size(axes)
    after = lax.ppermute(array[1], axes, [(i + 1, i) for i in range(count - 1)])
    before = lax.ppermute(array[0], axes, [(i, i + 1) for i in range(count - 1)])
    return after, before


def pick_kernel(fields_ref, cols_ref, out_ref, table_ref):
    nfield, ncol = fields_ref.shape
    high = ncol // 256

    @pl.when(pl.program_id(0) == 0)
    def _():
        rows = [fields_ref[:, h * 256 : (h + 1) * 256].astype(F32) for h in range(high)]
        table_ref[...] = jnp.concatenate(rows, axis=0).astype(BF16)

    cols = cols_ref[0]
    width = cols.shape[1]
    low = cols & 255
    upper = cols >> 8
    onehot = jnp.where(lax.broadcasted_iota(jnp.int32, (256, width), 0) == low, 1.0, 0.0).astype(BF16)
    both = jnp.dot(table_ref[...], onehot, preferred_element_type=F32)
    picked = both[:nfield]
    for h in range(1, high):
        picked = jnp.where(upper == h, both[h * nfield : (h + 1) * nfield], picked)
    out_ref[0] = picked.astype(BF16)


def pick(fields, cols):
    groups, _, width = cols.shape
    nfield, ncol = fields.shape
    return pl.pallas_call(
        pick_kernel,
        grid=(groups,),
        in_specs=[
            pl.BlockSpec((nfield, ncol), lambda c: (0, 0)),
            pl.BlockSpec((1, 1, width), lambda c: (c, 0, 0)),
        ],
        out_specs=pl.BlockSpec((1, nfield, width), lambda c: (c, 0, 0)),
        out_shape=jax.ShapeDtypeStruct((groups, nfield, width), BF16),
        scratch_shapes=[pltpu.VMEM((nfield * (ncol // 256), 256), BF16)],
        compiler_params=params(),
    )(fields, cols)


def remap_kernel(live_ref, picked_ref, weights_ref, cells_ref, depth_ref, flux_ref, push_ref, spread_ref, total_ref):
    step = pl.program_id(0)
    nfield = picked_ref.shape[1]
    blocks = weights_ref.shape[1]
    live = live_ref[step]
    cells = cells_ref[0]
    picked = picked_ref[0]
    lows = []
    for k in range(blocks):
        part = slice(k * 256, (k + 1) * 256)
        contrib = lax.dot_general(
            picked[:, part], weights_ref[0, k], (((1,), (1,)), ((), ())), preferred_element_type=F32
        )
        big = contrib.astype(BF16).astype(F32)
        pair = jnp.concatenate([big, contrib - big], axis=0).astype(BF16)
        cell = cells[:, part]
        alive = jnp.int32(k) < live
        upper = jnp.where(alive, (cell >> 7) & 15, -1)
        for h in range(16):
            spread_ref[h * 2 * nfield : (h + 1) * 2 * nfield, part] = jnp.where(upper == h, pair, jnp.zeros_like(pair))
    low = ((cells >> 11) << 7) | (cells & 127)
    width = cells.shape[1]
    onehot = jnp.where(lax.broadcasted_iota(jnp.int32, (256, width), 0) == low, 1.0, 0.0).astype(BF16)
    added = lax.dot_general(spread_ref[...], onehot, (((1,), (1,)), ((), ())), preferred_element_type=F32)

    @pl.when(step == 0)
    def _():
        total_ref[...] = added

    @pl.when(step > 0)
    def _():
        total_ref[...] += added

    @pl.when(step == pl.num_programs(0) - 1)
    def _():
        for h in range(16):
            base = h * 2 * nfield
            row = total_ref[base : base + nfield, :] + total_ref[base + nfield : base + 2 * nfield, :]
            flux_ref[:, h, :] = row[:, :128]
            flux_ref[:, h + 16, :] = row[:, 128:]
        depth = depth_ref[...]
        push_ref[0] = flux_ref[0] / depth
        push_ref[1] = flux_ref[1] / depth
        push_ref[2] = flux_ref[2]


def remap(live, picked, weights, cells, depth):
    groups, nfield, width = picked.shape
    blocks = weights.shape[1]
    rows, cols = depth.shape
    return pl.pallas_call(
        remap_kernel,
        grid_spec=pltpu.PrefetchScalarGridSpec(
            num_scalar_prefetch=1,
            grid=(groups,),
            in_specs=[
                pl.BlockSpec((1, nfield, width), lambda c, live: (c, 0, 0)),
                pl.BlockSpec((1, blocks, 256, 256), lambda c, live: (c, 0, 0, 0)),
                pl.BlockSpec((1, 1, width), lambda c, live: (c, 0, 0)),
                pl.BlockSpec((rows, cols), lambda c, live: (0, 0)),
            ],
            out_specs=[
                pl.BlockSpec((nfield, rows, cols), lambda c, live: (0, 0, 0)),
                pl.BlockSpec((3, rows, cols), lambda c, live: (0, 0, 0)),
            ],
            scratch_shapes=[
                pltpu.VMEM((32 * nfield, width), BF16),
                pltpu.VMEM((32 * nfield, 256), F32),
            ],
        ),
        out_shape=[
            jax.ShapeDtypeStruct((nfield, rows, cols), F32),
            jax.ShapeDtypeStruct((3, rows, cols), F32),
        ],
        compiler_params=params(),
    )(live, picked, weights, cells, depth)


def sides(east, west):
    lane = lax.broadcasted_iota(jnp.int32, east.shape, east.ndim - 1)
    return jnp.where(lane < 64, east, west)


def edges_kernel(own_ref, east_ref, west_ref, top_ref, bottom_ref):
    rows = own_ref.shape[1]
    for ref, part in ((top_ref, slice(0, EDGE)), (bottom_ref, slice(rows - EDGE, rows))):
        ref[:, :, :128] = own_ref[:, part, :]
        ref[:, :, 128:] = sides(east_ref[:, part, :], west_ref[:, part, :])


def edge_rows(own, east, west):
    shape = jax.ShapeDtypeStruct((own.shape[0], EDGE, 256), F32)
    return pl.pallas_call(edges_kernel, out_shape=[shape, shape], compiler_params=params())(own, east, west)


def extend(out_ref, at, own, east, west, after, before):
    rows = own.shape[0]
    out_ref[at, :rows, :128] = own
    out_ref[at, :rows, 128:] = sides(east, west)
    out_ref[at, rows : rows + EDGE, :] = after
    out_ref[at, rows + EDGE :, :] = before


def halo(own):
    east, west = neighbours((own, own), ("comp",))
    top, bottom = edge_rows(own, east, west)
    after, before = neighbours((bottom, top), DOM)
    return east, west, after, before


def speed_kernel(depth_ref, wet_ref, level_ref, east_ref, north_ref, state_ref, peak_ref):
    wet = wet_ref[...].astype(F32)
    state_ref[0] = depth_ref[...]
    state_ref[1] = wet
    state_ref[2] = level_ref[...]
    state_ref[3] = east_ref[...]
    state_ref[4] = north_ref[...]
    speed = jnp.sqrt(depth_ref[...]) + wet * (jnp.abs(east_ref[...]) + jnp.abs(north_ref[...]))
    peak_ref[...] = jnp.broadcast_to(jnp.max(speed, keepdims=True), peak_ref.shape)


def static_kernel(own_ref, east_ref, west_ref, after_ref, before_ref, out_ref):
    for at in range(own_ref.shape[0]):
        extend(out_ref, at, own_ref[at], east_ref[at], west_ref[at], after_ref[at], before_ref[at])


def subcycle(first_row, total_rows, depth, wet, level, east, north, push_x, push_y, fresh, peak):
    nrow, ncol = depth.shape
    rows = nrow - 2 * EDGE
    step_dt = courant / peak
    row = lax.broadcasted_iota(jnp.int32, depth.shape, 0)
    row = first_row + jnp.where(row < rows + EDGE, row, row - nrow)
    rotation = 0.1 + 0.4 * (row.astype(F32) + 0.5) / total_rows

    def across(x):
        return pltpu.roll(x, ncol - 1, 1) - pltpu.roll(x, 1, 1)

    def along(x):
        return pltpu.roll(x, nrow - 1, 0) - pltpu.roll(x, 1, 0)

    flux_x = depth * east * wet
    flux_y = depth * north * wet
    diverge = 0.5 * (across(flux_x) + along(flux_y))
    level = wet * (level + step_dt * (fresh - diverge))
    grad_x = 0.5 * across(level)
    grad_y = 0.5 * along(level)
    new_east = wet * (east + step_dt * (rotation * north - grad_x + push_x - friction * east))
    new_north = wet * (north + step_dt * (-rotation * east - grad_y + push_y - friction * north))
    return level, new_east, new_north


def finish(depth, wet, level, east, north, state_ref, peak_ref):
    state_ref[0] = level
    state_ref[1] = east
    state_ref[2] = north
    rows = depth.shape[0] - 2 * EDGE
    own = (slice(0, rows), slice(0, 128))
    speed = jnp.sqrt(depth[own]) + wet[own] * (jnp.abs(east[own]) + jnp.abs(north[own]))
    peak_ref[...] = jnp.broadcast_to(jnp.max(speed, keepdims=True), peak_ref.shape)


def first_kernel(total_rows, row_ref, static_ref, own_ref, east_ref, west_ref, after_ref, before_ref, seen_ref, force_ref, state_ref, peak_ref):
    for at in range(3):
        extend(force_ref, at, own_ref[at], east_ref[at], west_ref[at], after_ref[at], before_ref[at])
    peak = jnp.max(seen_ref[...], keepdims=True)
    depth, wet = static_ref[0], static_ref[1]
    new = subcycle(
        row_ref[0], total_rows, depth, wet, static_ref[2], static_ref[3], static_ref[4],
        force_ref[0], force_ref[1], force_ref[2], peak,
    )
    finish(depth, wet, *new, state_ref, peak_ref)


def middle_kernel(total_rows, row_ref, static_ref, force_ref, old_ref, seen_ref, state_ref, peak_ref):
    peak = jnp.max(seen_ref[...], keepdims=True)
    depth, wet = static_ref[0], static_ref[1]
    new = subcycle(
        row_ref[0], total_rows, depth, wet, old_ref[0], old_ref[1], old_ref[2],
        force_ref[0], force_ref[1], force_ref[2], peak,
    )
    finish(depth, wet, *new, state_ref, peak_ref)


def last_kernel(total_rows, row_ref, static_ref, force_ref, old_ref, seen_ref, out_ref):
    peak = jnp.max(seen_ref[...], keepdims=True)
    new = subcycle(
        row_ref[0], total_rows, static_ref[0], static_ref[1], old_ref[0], old_ref[1], old_ref[2],
        force_ref[0], force_ref[1], force_ref[2], peak,
    )
    rows = out_ref.shape[1]
    for at in range(3):
        out_ref[at] = new[at][:rows, :128]


def call_small(kernel, scalars, arrays, out_shape):
    smem = [pl.BlockSpec(memory_space=pltpu.SMEM)] * len(scalars)
    vmem = [pl.BlockSpec(memory_space=pltpu.VMEM)] * len(arrays)
    return pl.pallas_call(kernel, in_specs=smem + vmem, out_shape=out_shape, compiler_params=params())(*scalars, *arrays)


def largest(peak):
    seen = lax.all_to_all(peak, PLANE, split_axis=0, concat_axis=0, tiled=True)
    second = jnp.broadcast_to(jnp.max(seen, axis=0, keepdims=True), (axes_size(COLUMN), 128))
    return lax.all_to_all(second, COLUMN, split_axis=0, concat_axis=0, tiled=True)


def shards(
    atm_fields,
    send_cols,
    live_blocks,
    remap_weights,
    row_map,
    ocean_depth,
    wet_mask,
    sea_level,
    east_vel,
    north_vel,
):
    groups = send_cols.shape[2]
    rows, cols = ocean_depth.shape
    total_rows = rows * axes_size(DOM)
    first_row = (lax.axis_index(DOM) * rows).reshape(1).astype(jnp.int32)
    peak_shape = jax.ShapeDtypeStruct((axes_size(PLANE), 128), F32)
    wide = (rows + 2 * EDGE, 2 * cols)

    picked = pick(atm_fields, send_cols.reshape(groups, 1, -1))
    own, peak = call_small(
        speed_kernel, (), (ocean_depth, wet_mask, sea_level, east_vel, north_vel),
        [jax.ShapeDtypeStruct((5, rows, cols), F32), peak_shape],
    )
    received = lax.all_to_all(picked, "comp", split_axis=0, concat_axis=0, tiled=True)
    seen = largest(peak)
    static = call_small(static_kernel, (), (own, *halo(own)), jax.ShapeDtypeStruct((5, *wide), F32))
    fluxes, push = remap(live_blocks.reshape(groups), received, remap_weights[0, 0], row_map.reshape(groups, 1, -1), ocean_depth)
    three = jax.ShapeDtypeStruct((3, *wide), F32)
    force, state, peak = call_small(
        functools.partial(first_kernel, total_rows), (first_row,), (static, push, *halo(push), seen), [three, three, peak_shape]
    )
    for _ in range(NSUB - 2):
        seen = largest(peak)
        state, peak = call_small(
            functools.partial(middle_kernel, total_rows), (first_row,), (static, force, state, seen), [three, peak_shape]
        )
    seen = largest(peak)
    state = call_small(
        functools.partial(last_kernel, total_rows), (first_row,), (static, force, state, seen),
        jax.ShapeDtypeStruct((3, rows, cols), F32),
    )
    return fluxes, state


def solution(mesh):
    split = Mesh(mesh.devices.reshape(mesh.shape["comp"], *DOM_SHAPE), COMP_DOM)
    return jax.shard_map(
        shards,
        mesh=split,
        in_specs=(
            P(None, COMP_DOM),
            P("comp", DOM, None, None, None),
            P("comp", DOM, None),
            P("comp", DOM, None, None, None, None),
            P("comp", DOM, None, None, None),
            P(DOM, "comp"),
            P(DOM, "comp"),
            P(DOM, "comp"),
            P(DOM, "comp"),
            P(DOM, "comp"),
        ),
        out_specs=(P(None, DOM, "comp"), P(None, DOM, "comp")),
        check_vma=False,
    )
```

```python
import functools

import jax
import jax.numpy as jnp
from jax import lax
from jax.experimental import pallas as pl
from jax.experimental.pallas import tpu as pltpu
from jax.sharding import Mesh
from jax.sharding import PartitionSpec as P

NSUB = 4
DOM_SHAPE = (12, 4, 2)
COMP_DOM = ("comp", "dom_0", "dom_1", "dom_2")
DOM = ("dom_0", "dom_1", "dom_2")
PLANE = ("comp", "dom_1")
COLUMN = ("dom_0", "dom_2")
BF16 = jnp.bfloat16
F32 = jnp.float32

courant = 0.5
friction = 0.05

EDGE = 8
KEPT = 8
HIGH = 8
NT = (((1,), (1,)), ((), ()))
HBM = pl.BlockSpec(memory_space=pltpu.HBM)
SMEM = pl.BlockSpec(memory_space=pltpu.SMEM)
VMEM = pl.BlockSpec(memory_space=pltpu.VMEM)


def params(mib):
    return pltpu.CompilerParams(vmem_limit_bytes=mib * 1024 * 1024)


def axes_size(axes):
    return functools.reduce(lambda a, b: a * b, [lax.axis_size(a) for a in axes])


def neighbours(head, tail, axes):
    count = axes_size(axes)
    after = lax.ppermute(head, axes, [(i + 1, i) for i in range(count - 1)])
    before = lax.ppermute(tail, axes, [(i, i + 1) for i in range(count - 1)])
    return after, before


def fetch(refs, buffers, sems, first=0):
    copies = [pltpu.make_async_copy(ref, buf, sems.at[first + i]) for i, (ref, buf) in enumerate(zip(refs, buffers))]
    for copy in copies:
        copy.start()
    return copies


def rows16(row, count):
    tile = jnp.broadcast_to(row.astype(F32), (16, row.shape[1])).astype(BF16)
    return jnp.concatenate([tile] * (count // 16), axis=0)


def onehot(row, count):
    at = lax.broadcasted_iota(jnp.int32, (count, row.shape[1]), 0).astype(F32).astype(BF16)
    return jnp.where(at == rows16(row, count), jnp.ones_like(at), jnp.zeros_like(at))


def pick_kernel(fields_hbm, cols_hbm, out_ref, fields_ref, cols_ref, sems):
    for copy in fetch((fields_hbm, cols_hbm), (fields_ref, cols_ref), sems):
        copy.wait()
    nfield, ncol = fields_ref.shape
    high = ncol // 256
    rows = [fields_ref[:, h * 256 : (h + 1) * 256].astype(F32) for h in range(high)]
    table = jnp.concatenate(rows, axis=0).astype(BF16)
    groups, blocks, width = cols_ref.shape[2:]
    for c in range(groups):
        for k in range(blocks):
            cols = cols_ref[0, 0, c, k : k + 1, :]
            both = jnp.dot(table, onehot(cols & 255, 256), preferred_element_type=F32)
            upper = jnp.broadcast_to(cols >> 8, (nfield, width))
            picked = both[:nfield]
            for h in range(1, high):
                picked = jnp.where(upper == h, both[h * nfield : (h + 1) * nfield], picked)
            out_ref[c, :, k * width : (k + 1) * width] = picked.astype(BF16)


def pick(fields, cols):
    groups, blocks, width = cols.shape[2:]
    return pl.pallas_call(
        pick_kernel,
        grid=(1,),
        in_specs=[HBM, HBM],
        out_specs=pl.BlockSpec((groups, fields.shape[0], blocks * width), lambda i: (0, 0, 0)),
        out_shape=jax.ShapeDtypeStruct((groups, fields.shape[0], blocks * width + 128), BF16),
        scratch_shapes=[
            pltpu.VMEM(fields.shape, BF16),
            pltpu.VMEM(cols.shape, jnp.int32),
            pltpu.SemaphoreType.DMA((2,)),
        ],
        compiler_params=params(56),
    )(fields, cols)


def peak_of(depth, wet, east, north):
    return jnp.max(jnp.sqrt(depth) + wet * (jnp.abs(east) + jnp.abs(north)), keepdims=True)


def speed_kernel(depth_hbm, wet_hbm, east_hbm, north_hbm, peak_ref, real_ref, wet_ref, sems):
    copies = fetch(
        (depth_hbm, east_hbm, north_hbm, wet_hbm), (real_ref.at[0], real_ref.at[1], real_ref.at[2], wet_ref), sems
    )
    for copy in copies:
        copy.wait()
    peak = peak_of(real_ref[0], wet_ref[...].astype(F32), real_ref[1], real_ref[2])
    peak_ref[...] = jnp.broadcast_to(peak, peak_ref.shape)


def first_speed(depth, wet, east, north):
    return pl.pallas_call(
        speed_kernel,
        in_specs=[HBM] * 4,
        out_specs=VMEM,
        out_shape=jax.ShapeDtypeStruct((axes_size(DOM), 128), F32),
        scratch_shapes=[
            pltpu.VMEM((3, *depth.shape), F32),
            pltpu.VMEM(depth.shape, jnp.int32),
            pltpu.SemaphoreType.DMA((4,)),
        ],
        compiler_params=params(56),
    )(depth, wet, east, north)


def exchange(peak, axes):
    return lax.all_to_all(peak, axes, split_axis=0, concat_axis=0, tiled=True)


def insert_kernel(seen_ref, picked_ref, out_ref):
    peak = jnp.broadcast_to(jnp.max(seen_ref[...], keepdims=True), (1, 128))
    big = peak.astype(BF16).astype(F32)
    middle = (peak - big).astype(BF16).astype(F32)
    row = lax.broadcasted_iota(jnp.int32, out_ref.shape[1:], 0)
    three = jnp.where(row == 0, big, jnp.where(row == 1, middle, jnp.where(row == 2, peak - big - middle, 0.0)))
    for c in range(out_ref.shape[0]):
        out_ref[c] = three.astype(BF16)


def insert(seen, picked):
    groups, nfield, width = picked.shape
    return pl.pallas_call(
        insert_kernel,
        grid=(1,),
        in_specs=[pl.BlockSpec(seen.shape, lambda i: (0, 0)), HBM],
        out_specs=pl.BlockSpec((groups, nfield, 128), lambda i: (0, 0, width // 128 - 1)),
        out_shape=jax.ShapeDtypeStruct(picked.shape, picked.dtype),
        input_output_aliases={1: 0},
        compiler_params=params(56),
    )(seen, picked)


def spread_max(seen, axes):
    return jnp.broadcast_to(jnp.max(seen, axis=0, keepdims=True), (axes_size(axes), 128))


def remap_kernel(
    live_ref, picked_hbm, weights_hbm, cells_hbm, depth_hbm, wet_hbm, level_hbm, east_hbm, north_hbm,
    flux_ref, own_ref, head_ref, tail_ref, peak_ref,
    picked_ref, weights_ref, cells_ref, wet_ref, spread_ref, total_ref, sems,
):
    groups, nfield, width = picked_ref.shape
    blocks = weights_ref.shape[1]
    pair_rows = 2 * nfield
    lows = total_ref.shape[1]
    first = fetch((picked_hbm, cells_hbm), (picked_ref, cells_ref), sems)
    loads = fetch([weights_hbm.at[0, 0, c] for c in range(groups)], [weights_ref.at[c] for c in range(groups)], sems, 2)
    rest = fetch(
        (depth_hbm, level_hbm, east_hbm, north_hbm, wet_hbm),
        (own_ref.at[0], own_ref.at[2], own_ref.at[3], own_ref.at[4], wet_ref),
        sems,
        2 + groups,
    )
    for copy in first:
        copy.wait()
    peak = None
    for c in range(groups):
        three = picked_ref[c, :, blocks * 256 :].astype(F32)
        one = three[0:1] + (three[1:2] + three[2:3])
        peak = one if peak is None else jnp.maximum(peak, one)
    peak_ref[...] = jnp.broadcast_to(peak, peak_ref.shape)
    for c in range(groups):
        loads[c].wait()
        live = live_ref[0, 0, c]
        onehots = []
        for k in range(blocks):
            part = slice(k * 256, (k + 1) * 256)
            contrib = lax.dot_general(picked_ref[c, :, part], weights_ref[c, k], NT, preferred_element_type=F32)
            big = contrib.astype(BF16).astype(F32)
            pair = jnp.concatenate([big, contrib - big], axis=0).astype(BF16)
            cell = cells_ref[0, 0, c, k : k + 1, :]
            upper = rows16(jnp.where(jnp.int32(k) < live, (cell >> 7) & (HIGH - 1), -1), pair_rows)
            for h in range(HIGH):
                spread_ref[h * pair_rows : (h + 1) * pair_rows, part] = jnp.where(
                    upper == BF16(h), pair, jnp.zeros_like(pair)
                )
            row, column = cell >> 7, cell & 127
            low = (row // HIGH) * 128 + column
            tiles = [onehot(jnp.where(low >> 8 == t, low & 255, -1), 256) for t in range(lows // 256)]
            onehots.append(jnp.concatenate(tiles, axis=0))
        added = lax.dot_general(
            spread_ref[...], jnp.concatenate(onehots, axis=1), NT, preferred_element_type=F32
        )
        if c == 0:
            total_ref[...] = added
        else:
            total_ref[...] += added
    for h in range(HIGH):
        base = h * pair_rows
        both = total_ref[base : base + nfield, :] + total_ref[base + nfield : base + pair_rows, :]
        for r in range(lows // 128):
            flux_ref[:, r * HIGH + h, :] = both[:, r * 128 : (r + 1) * 128]
    for copy in rest:
        copy.wait()
    own_ref[1] = wet_ref[...].astype(F32)
    own_ref[5] = flux_ref[0] / own_ref[0]
    own_ref[6] = flux_ref[1] / own_ref[0]
    own_ref[7] = flux_ref[2]
    lane = lax.broadcasted_iota(jnp.int32, head_ref.shape, 1)
    head = own_ref[0]
    tail = pltpu.roll(own_ref[0], EDGE, 1)
    for at in range(1, KEPT):
        here = lane // EDGE == at
        head = jnp.where(here, pltpu.roll(own_ref[at], at * EDGE, 1), head)
        tail = jnp.where(here, pltpu.roll(own_ref[at], (at + 1) * EDGE, 1), tail)
    head_ref[...] = head
    tail_ref[...] = tail


def remap(live, picked, weights, cells, depth, wet, level, east, north):
    groups, nfield, width = picked.shape
    rows, cols = depth.shape
    tile = jax.ShapeDtypeStruct((rows, cols), F32)
    return pl.pallas_call(
        remap_kernel,
        in_specs=[SMEM] + [HBM] * 8,
        out_specs=[VMEM] * 5,
        out_shape=[
            jax.ShapeDtypeStruct((nfield, rows, cols), F32),
            jax.ShapeDtypeStruct((KEPT, rows, cols), F32),
            tile,
            tile,
            jax.ShapeDtypeStruct((8, 128), F32),
        ],
        scratch_shapes=[
            pltpu.VMEM(picked.shape, BF16),
            pltpu.VMEM(weights.shape[2:], BF16),
            pltpu.VMEM(cells.shape, jnp.int32),
            pltpu.VMEM((rows, cols), jnp.int32),
            pltpu.VMEM((HIGH * 2 * nfield, cells.shape[3] * cells.shape[4]), BF16),
            pltpu.VMEM((HIGH * 2 * nfield, rows // HIGH * cols), F32),
            pltpu.SemaphoreType.DMA((groups + 7,)),
        ],
        compiler_params=params(56),
    )(live, picked, weights, cells, depth, wet, level, east, north)


def edges_kernel(own_ref, east_ref, west_ref, top_ref, bottom_ref):
    rows = own_ref.shape[1]
    for ref, part in ((top_ref, slice(0, EDGE)), (bottom_ref, slice(rows - EDGE, rows))):
        ref[:KEPT] = own_ref[:, part, :]
        ref[KEPT] = east_ref[part, :]
        ref[KEPT + 1] = west_ref[part, :]


def beside(at, east, west):
    lane = lax.broadcasted_iota(jnp.int32, east.shape, 1)
    return jnp.where(
        lane < 64,
        pltpu.roll(east, (128 - at * EDGE) % 128, 1),
        pltpu.roll(west, (128 - EDGE - at * EDGE) % 128, 1),
    )


def extended(at, own_ref, east_ref, west_ref, after_ref, before_ref):
    left = jnp.concatenate([own_ref[at], after_ref[at], before_ref[at]], axis=0)
    right = [beside(at, east_ref[...], west_ref[...])]
    right += [beside(at, ref[KEPT], ref[KEPT + 1]) for ref in (after_ref, before_ref)]
    return jnp.concatenate([left, jnp.concatenate(right, axis=0)], axis=1)


def subcycle(first_row, total_rows, depth, wet, level, east, north, push_x, push_y, fresh, peak):
    nrow, ncol = depth.shape
    rows = nrow - 2 * EDGE
    step_dt = courant / peak
    row = lax.broadcasted_iota(jnp.int32, depth.shape, 0)
    row = first_row + jnp.where(row < rows + EDGE, row, row - nrow)
    rotation = 0.1 + 0.4 * (row.astype(F32) + 0.5) / total_rows

    def across(x):
        return pltpu.roll(x, ncol - 1, 1) - pltpu.roll(x, 1, 1)

    def along(x):
        return pltpu.roll(x, nrow - 1, 0) - pltpu.roll(x, 1, 0)

    flux_x = depth * east * wet
    flux_y = depth * north * wet
    diverge = 0.5 * (across(flux_x) + along(flux_y))
    level = wet * (level + step_dt * (fresh - diverge))
    grad_x = 0.5 * across(level)
    grad_y = 0.5 * along(level)
    new_east = wet * (east + step_dt * (rotation * north - grad_x + push_x - friction * east))
    new_north = wet * (north + step_dt * (-rotation * east - grad_y + push_y - friction * north))
    return level, new_east, new_north


def finish(depth, wet, new, state_ref, peak_ref):
    for at in range(3):
        state_ref[at] = new[at]
    own = (slice(0, depth.shape[0] - 2 * EDGE), slice(0, 128))
    peak = peak_of(depth[own], wet[own], new[1][own], new[2][own])
    peak_ref[...] = jnp.broadcast_to(peak, peak_ref.shape)


def first_kernel(
    total_rows, row_ref, own_ref, east_ref, west_ref, after_ref, before_ref, seen_ref, kept_ref, state_ref, peak_ref
):
    full = [extended(at, own_ref, east_ref, west_ref, after_ref, before_ref) for at in range(KEPT)]
    depth, wet, level, east, north, push_x, push_y, fresh = full
    for at, array in enumerate((depth, wet, push_x, push_y, fresh)):
        kept_ref[at] = array
    peak = jnp.max(seen_ref[...], keepdims=True)
    finish(depth, wet, subcycle(row_ref[0], total_rows, *full, peak), state_ref, peak_ref)


def next_state(total_rows, row_ref, kept_ref, old_ref, seen_ref):
    peak = jnp.max(seen_ref[...], keepdims=True)
    return subcycle(
        row_ref[0], total_rows, kept_ref[0], kept_ref[1], old_ref[0], old_ref[1], old_ref[2],
        kept_ref[2], kept_ref[3], kept_ref[4], peak,
    )


def middle_kernel(total_rows, row_ref, kept_ref, old_ref, seen_ref, state_ref, peak_ref):
    new = next_state(total_rows, row_ref, kept_ref, old_ref, seen_ref)
    finish(kept_ref[0], kept_ref[1], new, state_ref, peak_ref)


def last_kernel(total_rows, row_ref, kept_ref, old_ref, seen_ref, out_ref):
    new = next_state(total_rows, row_ref, kept_ref, old_ref, seen_ref)
    for at in range(3):
        out_ref[at] = new[at][: out_ref.shape[1], :128]


def call_small(kernel, scalars, arrays, out_shape):
    return pl.pallas_call(
        kernel, in_specs=[SMEM] * len(scalars) + [VMEM] * len(arrays), out_shape=out_shape, compiler_params=params(8)
    )(*scalars, *arrays)


def shards(
    atm_fields,
    send_cols,
    live_blocks,
    remap_weights,
    row_map,
    ocean_depth,
    wet_mask,
    sea_level,
    east_vel,
    north_vel,
):
    rows, cols = ocean_depth.shape
    total_rows = rows * axes_size(DOM)
    first_row = (lax.axis_index(DOM) * rows).reshape(1).astype(jnp.int32)
    wide = (rows + 2 * EDGE, 2 * cols)
    three = jax.ShapeDtypeStruct((3, *wide), F32)
    five = jax.ShapeDtypeStruct((5, *wide), F32)
    rim = jax.ShapeDtypeStruct((KEPT + 2, EDGE, cols), F32)
    peak_shape = jax.ShapeDtypeStruct((axes_size(PLANE), 128), F32)

    seen = exchange(first_speed(ocean_depth, wet_mask, east_vel, north_vel), DOM)
    picked = pick(atm_fields, send_cols)
    picked = insert(seen, picked)
    received = lax.all_to_all(picked, "comp", split_axis=0, concat_axis=0, tiled=True)
    fluxes, own, head, tail, seen = remap(
        live_blocks, received, remap_weights, row_map, ocean_depth, wet_mask, sea_level, east_vel, north_vel
    )
    east, west = neighbours(head, tail, ("comp",))
    top, bottom = call_small(edges_kernel, (), (own, east, west), [rim, rim])
    after, before = neighbours(top, bottom, DOM)
    kept, state, peak = call_small(
        functools.partial(first_kernel, total_rows),
        (first_row,),
        (own, east, west, after, before, seen),
        [five, three, peak_shape],
    )
    for substep in range(1, NSUB):
        seen = exchange(spread_max(exchange(peak, PLANE), COLUMN), COLUMN)
        if substep < NSUB - 1:
            state, peak = call_small(
                functools.partial(middle_kernel, total_rows), (first_row,), (kept, state, seen), [three, peak_shape]
            )
    state = call_small(
        functools.partial(last_kernel, total_rows), (first_row,), (kept, state, seen),
        jax.ShapeDtypeStruct((3, rows, cols), F32),
    )
    return fluxes, state


def solution(mesh):
    split = Mesh(mesh.devices.reshape(mesh.shape["comp"], *DOM_SHAPE), COMP_DOM)
    return jax.shard_map(
        shards,
        mesh=split,
        in_specs=(
            P(None, COMP_DOM),
            P("comp", DOM, None, None, None),
            P("comp", DOM, None),
            P("comp", DOM, None, None, None, None),
            P("comp", DOM, None, None, None),
            P(DOM, "comp"),
            P(DOM, "comp"),
            P(DOM, "comp"),
            P(DOM, "comp"),
            P(DOM, "comp"),
        ),
        out_specs=(P(None, DOM, "comp"), P(None, DOM, "comp")),
        check_vma=False,
    )
```

```python
import functools

import jax
import jax.numpy as jnp
from jax import lax
from jax.experimental import pallas as pl
from jax.experimental.pallas import tpu as pltpu
from jax.sharding import Mesh
from jax.sharding import PartitionSpec as P

DOM_SHAPE = (12, 4, 2)
COMP_DOM = ("comp", "dom_0", "dom_1", "dom_2")
DOM = ("dom_0", "dom_1", "dom_2")
PLANE = ("comp", "dom_1")
COLUMN = ("dom_0", "dom_2")
BF16 = jnp.bfloat16
F32 = jnp.float32

courant = 0.5
friction = 0.05

EDGE = 8
KEPT = 8
HIGH = 8
NT = (((1,), (1,)), ((), ()))
HBM = pl.BlockSpec(memory_space=pltpu.HBM)
SMEM = pl.BlockSpec(memory_space=pltpu.SMEM)
VMEM = pl.BlockSpec(memory_space=pltpu.VMEM)


def params(mib):
    return pltpu.CompilerParams(vmem_limit_bytes=mib * 1024 * 1024)


def axes_size(axes):
    return functools.reduce(lambda a, b: a * b, [lax.axis_size(a) for a in axes])


def neighbours(head, tail, axes):
    count = axes_size(axes)
    after = lax.ppermute(head, axes, [(i + 1, i) for i in range(count - 1)])
    before = lax.ppermute(tail, axes, [(i, i + 1) for i in range(count - 1)])
    return after, before


def fetch(refs, buffers, sems, first=0):
    copies = [pltpu.make_async_copy(ref, buf, sems.at[first + i]) for i, (ref, buf) in enumerate(zip(refs, buffers))]
    for copy in copies:
        copy.start()
    return copies


def rows16(row, count):
    tile = jnp.broadcast_to(row.astype(F32), (16, row.shape[1])).astype(BF16)
    return jnp.concatenate([tile] * (count // 16), axis=0)


def onehot(row, count):
    at = lax.broadcasted_iota(jnp.int32, (count, row.shape[1]), 0).astype(F32).astype(BF16)
    return jnp.where(at == rows16(row, count), jnp.ones_like(at), jnp.zeros_like(at))


def pick_kernel(fields_hbm, cols_hbm, out_ref, fields_ref, cols_ref, sems):
    for copy in fetch((fields_hbm, cols_hbm), (fields_ref, cols_ref), sems):
        copy.wait()
    nfield, ncol = fields_ref.shape
    high = ncol // 256
    rows = [fields_ref[:, h * 256 : (h + 1) * 256].astype(F32) for h in range(high)]
    table = jnp.concatenate(rows, axis=0).astype(BF16)
    groups, blocks, width = cols_ref.shape[2:]
    for c in range(groups):
        for k in range(blocks):
            cols = cols_ref[0, 0, c, k : k + 1, :]
            both = jnp.dot(table, onehot(cols & 255, 256), preferred_element_type=F32)
            upper = jnp.broadcast_to(cols >> 8, (nfield, width))
            picked = both[:nfield]
            for h in range(1, high):
                picked = jnp.where(upper == h, both[h * nfield : (h + 1) * nfield], picked)
            out_ref[c, :, k * width : (k + 1) * width] = picked.astype(BF16)


def pick(fields, cols):
    groups, blocks, width = cols.shape[2:]
    return pl.pallas_call(
        pick_kernel,
        grid=(1,),
        in_specs=[HBM, HBM],
        out_specs=pl.BlockSpec((groups, fields.shape[0], blocks * width), lambda i: (0, 0, 0)),
        out_shape=jax.ShapeDtypeStruct((groups, fields.shape[0], blocks * width + 128), BF16),
        scratch_shapes=[
            pltpu.VMEM(fields.shape, BF16),
            pltpu.VMEM(cols.shape, jnp.int32),
            pltpu.SemaphoreType.DMA((2,)),
        ],
        compiler_params=params(56),
    )(fields, cols)


def peak_of(depth, wet, east, north):
    return jnp.max(jnp.sqrt(depth) + wet * (jnp.abs(east) + jnp.abs(north)), keepdims=True)


def speed_kernel(depth_hbm, wet_hbm, east_hbm, north_hbm, peak_ref, real_ref, wet_ref, sems):
    copies = fetch(
        (depth_hbm, east_hbm, north_hbm, wet_hbm), (real_ref.at[0], real_ref.at[1], real_ref.at[2], wet_ref), sems
    )
    for copy in copies:
        copy.wait()
    peak = peak_of(real_ref[0], wet_ref[...].astype(F32), real_ref[1], real_ref[2])
    peak_ref[...] = jnp.broadcast_to(peak, peak_ref.shape)


def first_speed(depth, wet, east, north):
    return pl.pallas_call(
        speed_kernel,
        in_specs=[HBM] * 4,
        out_specs=VMEM,
        out_shape=jax.ShapeDtypeStruct((axes_size(DOM), 128), F32),
        scratch_shapes=[
            pltpu.VMEM((3, *depth.shape), F32),
            pltpu.VMEM(depth.shape, jnp.int32),
            pltpu.SemaphoreType.DMA((4,)),
        ],
        compiler_params=params(56),
    )(depth, wet, east, north)


def exchange(peak, axes):
    return lax.all_to_all(peak, axes, split_axis=0, concat_axis=0, tiled=True)


def insert_kernel(seen_ref, picked_ref, out_ref):
    peak = jnp.broadcast_to(jnp.max(seen_ref[...], keepdims=True), (1, 128))
    big = peak.astype(BF16).astype(F32)
    middle = (peak - big).astype(BF16).astype(F32)
    row = lax.broadcasted_iota(jnp.int32, out_ref.shape[1:], 0)
    three = jnp.where(row == 0, big, jnp.where(row == 1, middle, jnp.where(row == 2, peak - big - middle, 0.0)))
    for c in range(out_ref.shape[0]):
        out_ref[c] = three.astype(BF16)


def insert(seen, picked):
    groups, nfield, width = picked.shape
    return pl.pallas_call(
        insert_kernel,
        grid=(1,),
        in_specs=[pl.BlockSpec(seen.shape, lambda i: (0, 0)), HBM],
        out_specs=pl.BlockSpec((groups, nfield, 128), lambda i: (0, 0, width // 128 - 1)),
        out_shape=jax.ShapeDtypeStruct(picked.shape, picked.dtype),
        input_output_aliases={1: 0},
        compiler_params=params(56),
    )(seen, picked)


def everyone(peak):
    return exchange(spread_max(exchange(peak, PLANE), COLUMN), COLUMN)


def spread_max(seen, axes):
    return jnp.broadcast_to(jnp.max(seen, axis=0, keepdims=True), (axes_size(axes), 128))


def remap_kernel(
    live_ref, picked_hbm, weights_hbm, cells_hbm, depth_hbm, wet_hbm, level_hbm, east_hbm, north_hbm,
    flux_ref, own_ref, head_ref, tail_ref, peak_ref,
    picked_ref, weights_ref, cells_ref, wet_ref, spread_ref, total_ref, sems,
):
    groups, nfield, width = picked_ref.shape
    blocks = weights_ref.shape[1]
    pair_rows = 2 * nfield
    lows = total_ref.shape[1]
    first = fetch((picked_hbm, cells_hbm), (picked_ref, cells_ref), sems)
    loads = fetch([weights_hbm.at[0, 0, c] for c in range(groups)], [weights_ref.at[c] for c in range(groups)], sems, 2)
    rest = fetch(
        (depth_hbm, level_hbm, east_hbm, north_hbm, wet_hbm),
        (own_ref.at[0], own_ref.at[2], own_ref.at[3], own_ref.at[4], wet_ref),
        sems,
        2 + groups,
    )
    for copy in first:
        copy.wait()
    peak = None
    for c in range(groups):
        three = picked_ref[c, :, blocks * 256 :].astype(F32)
        one = three[0:1] + (three[1:2] + three[2:3])
        peak = one if peak is None else jnp.maximum(peak, one)
    peak_ref[...] = jnp.broadcast_to(peak, peak_ref.shape)
    for c in range(groups):
        loads[c].wait()
        live = live_ref[0, 0, c]
        onehots = []
        for k in range(blocks):
            part = slice(k * 256, (k + 1) * 256)
            contrib = lax.dot_general(picked_ref[c, :, part], weights_ref[c, k], NT, preferred_element_type=F32)
            big = contrib.astype(BF16).astype(F32)
            pair = jnp.concatenate([big, contrib - big], axis=0).astype(BF16)
            cell = cells_ref[0, 0, c, k : k + 1, :]
            upper = rows16(jnp.where(jnp.int32(k) < live, (cell >> 7) & (HIGH - 1), -1), pair_rows)
            for h in range(HIGH):
                spread_ref[h * pair_rows : (h + 1) * pair_rows, part] = jnp.where(
                    upper == BF16(h), pair, jnp.zeros_like(pair)
                )
            row, column = cell >> 7, cell & 127
            low = (row // HIGH) * 128 + column
            tiles = [onehot(jnp.where(low >> 8 == t, low & 255, -1), 256) for t in range(lows // 256)]
            onehots.append(jnp.concatenate(tiles, axis=0))
        added = lax.dot_general(
            spread_ref[...], jnp.concatenate(onehots, axis=1), NT, preferred_element_type=F32
        )
        if c == 0:
            total_ref[...] = added
        else:
            total_ref[...] += added
    for h in range(HIGH):
        base = h * pair_rows
        both = total_ref[base : base + nfield, :] + total_ref[base + nfield : base + pair_rows, :]
        for r in range(lows // 128):
            flux_ref[:, r * HIGH + h, :] = both[:, r * 128 : (r + 1) * 128]
    for copy in rest:
        copy.wait()
    own_ref[1] = wet_ref[...].astype(F32)
    own_ref[5] = flux_ref[0] / own_ref[0]
    own_ref[6] = flux_ref[1] / own_ref[0]
    own_ref[7] = flux_ref[2]
    lane = lax.broadcasted_iota(jnp.int32, head_ref.shape, 1)
    head = own_ref[0]
    tail = pltpu.roll(own_ref[0], EDGE, 1)
    for at in range(1, KEPT):
        here = lane // EDGE == at
        head = jnp.where(here, pltpu.roll(own_ref[at], at * EDGE, 1), head)
        tail = jnp.where(here, pltpu.roll(own_ref[at], (at + 1) * EDGE, 1), tail)
    head_ref[...] = head
    tail_ref[...] = tail


def remap(live, picked, weights, cells, depth, wet, level, east, north):
    groups, nfield, width = picked.shape
    rows, cols = depth.shape
    tile = jax.ShapeDtypeStruct((rows, cols), F32)
    return pl.pallas_call(
        remap_kernel,
        in_specs=[SMEM] + [HBM] * 8,
        out_specs=[VMEM] * 5,
        out_shape=[
            jax.ShapeDtypeStruct((nfield, rows, cols), F32),
            jax.ShapeDtypeStruct((KEPT, rows, cols), F32),
            tile,
            tile,
            jax.ShapeDtypeStruct((8, 128), F32),
        ],
        scratch_shapes=[
            pltpu.VMEM(picked.shape, BF16),
            pltpu.VMEM(weights.shape[2:], BF16),
            pltpu.VMEM(cells.shape, jnp.int32),
            pltpu.VMEM((rows, cols), jnp.int32),
            pltpu.VMEM((HIGH * 2 * nfield, cells.shape[3] * cells.shape[4]), BF16),
            pltpu.VMEM((HIGH * 2 * nfield, rows // HIGH * cols), F32),
            pltpu.SemaphoreType.DMA((groups + 7,)),
        ],
        compiler_params=params(56),
    )(live, picked, weights, cells, depth, wet, level, east, north)


def edges_kernel(own_ref, east_ref, west_ref, top_ref, bottom_ref):
    rows = own_ref.shape[1]
    for ref, part in ((top_ref, slice(0, EDGE)), (bottom_ref, slice(rows - EDGE, rows))):
        ref[:KEPT] = own_ref[:, part, :]
        ref[KEPT] = east_ref[part, :]
        ref[KEPT + 1] = west_ref[part, :]


def beside(at, east, west):
    lane = lax.broadcasted_iota(jnp.int32, east.shape, 1)
    return jnp.where(
        lane < 64,
        pltpu.roll(east, (128 - at * EDGE) % 128, 1),
        pltpu.roll(west, (128 - EDGE - at * EDGE) % 128, 1),
    )


def extended(at, own_ref, east_ref, west_ref, after_ref, before_ref):
    left = jnp.concatenate([own_ref[at], after_ref[at], before_ref[at]], axis=0)
    right = [beside(at, east_ref[...], west_ref[...])]
    right += [beside(at, ref[KEPT], ref[KEPT + 1]) for ref in (after_ref, before_ref)]
    return jnp.concatenate([left, jnp.concatenate(right, axis=0)], axis=1)


def turning(first_row, total_rows, shape):
    row = lax.broadcasted_iota(jnp.int32, shape, 0)
    row = first_row + jnp.where(row < shape[0] - EDGE, row, row - shape[0])
    return 0.1 + 0.4 * (row.astype(F32) + 0.5) / total_rows


def subcycle(first_row, total_rows, depth, wet, level, east, north, push_x, push_y, fresh, peak):
    step_dt = courant / peak
    rotation = turning(first_row, total_rows, depth.shape)
    flux_x = depth * east * wet
    flux_y = depth * north * wet
    diverge = 0.5 * (across(flux_x) + along(flux_y))
    level = wet * (level + step_dt * (fresh - diverge))
    grad_x = 0.5 * across(level)
    grad_y = 0.5 * along(level)
    new_east = wet * (east + step_dt * (rotation * north - grad_x + push_x - friction * east))
    new_north = wet * (north + step_dt * (-rotation * east - grad_y + push_y - friction * north))
    return level, new_east, new_north


def across(x):
    return pltpu.roll(x, x.shape[1] - 1, 1) - pltpu.roll(x, 1, 1)


def along(x):
    return pltpu.roll(x, x.shape[0] - 1, 0) - pltpu.roll(x, 1, 0)


SAMPLES = (1.2, 0.8, 0.5, 0.3, 0.12)
CLOSE = 4e-6


def curve(terms, dt):
    root, east0, east1, east2, north0, north1, north2 = terms
    return root + jnp.abs(east0 + dt * (east1 + dt * east2)) + jnp.abs(north0 + dt * (north1 + dt * north2))


def offers(rotation, depth, wet, level, east, north, push_x, push_y, fresh, dt):
    drift = wet * (fresh - 0.5 * (across(depth * east * wet) + along(depth * north * wet)))
    still = wet * level
    own = (slice(0, depth.shape[0] - 2 * EDGE), slice(0, 128))
    terms = [
        term[own]
        for term in (
            jnp.sqrt(depth),
            wet * east,
            wet * (rotation * north - 0.5 * across(still) + push_x - friction * east),
            wet * (-0.5 * across(drift)),
            wet * north,
            wet * (-rotation * east - 0.5 * along(still) + push_y - friction * north),
            wet * (-0.5 * along(drift)),
        )
    ]
    shape = terms[0].shape
    index = lax.broadcasted_iota(jnp.int32, shape, 0) * 128 + lax.broadcasted_iota(jnp.int32, shape, 1)
    lane = lax.broadcasted_iota(jnp.int32, (1, 128), 1)
    row = jnp.where(lane == 0, peak_of(depth[own], wet[own], east[own], north[own]), 0.0)
    for j, ratio in enumerate(SAMPLES):
        speed = curve(terms, ratio * dt)
        fastest = speed == jnp.max(speed, keepdims=True)
        first = jnp.min(jnp.where(fastest, index, shape[0] * 128), keepdims=True)
        for i, term in enumerate(terms):
            value = jnp.sum(jnp.where(index == first, term, 0.0), keepdims=True)
            row = jnp.where(lane == 8 + 8 * j + i, value, row)
    return row


def offered(rows, dt):
    lane = lax.broadcasted_iota(jnp.int32, rows.shape, 1)
    terms = [rows] + [pltpu.roll(rows, 128 - i, 1) for i in range(1, 7)]
    here = (lane % 8 == 0) & (lane >= 8) & (lane < 8 + 8 * len(SAMPLES))
    return jnp.where(here, curve(terms, dt), 0.0)


def choose_kernel(rows_ref, seen_ref, out_ref):
    rows = rows_ref[...]
    count = rows.shape[0]
    lane = lax.broadcasted_iota(jnp.int32, rows.shape, 1)
    ratio = jnp.zeros(rows.shape, F32)
    for j, sample in enumerate(SAMPLES):
        ratio = jnp.where(lane // 8 == j + 1, sample, ratio)
    speed = offered(rows, ratio * (courant / jnp.max(seen_ref[...], keepdims=True)))
    number = lax.broadcasted_iota(jnp.int32, rows.shape, 0)
    best = jnp.min(jnp.where(speed == jnp.max(speed, axis=0, keepdims=True), number, count), axis=0, keepdims=True)
    chosen = jnp.where((number == best) & (lane % 8 == 0), 1.0, 0.0)
    for shift in (1, 2, 4):
        chosen = chosen + pltpu.roll(chosen, shift, 1)
    row = jnp.sum(jnp.where(chosen > 0.0, rows, 0.0), axis=0, keepdims=True)
    row = jnp.where(lane[:1] == 0, jnp.max(rows, axis=0, keepdims=True), row)
    out_ref[...] = jnp.broadcast_to(row, out_ref.shape)


def lane_max(rows, at):
    lane = lax.broadcasted_iota(jnp.int32, rows.shape, 1)
    return jnp.max(jnp.where(lane == at, rows, 0.0), keepdims=True)


def finish(depth, wet, new, state_ref, peak_ref):
    for at in range(3):
        state_ref[at] = new[at]
    own = (slice(0, depth.shape[0] - 2 * EDGE), slice(0, 128))
    return peak_of(depth[own], wet[own], new[1][own], new[2][own])


def first_kernel(
    total_rows, row_ref, own_ref, east_ref, west_ref, after_ref, before_ref, seen_ref, kept_ref, state_ref, peak_ref
):
    full = [extended(at, own_ref, east_ref, west_ref, after_ref, before_ref) for at in range(KEPT)]
    depth, wet, level, east, north, push_x, push_y, fresh = full
    for at, array in enumerate((depth, wet, push_x, push_y, fresh)):
        kept_ref[at] = array
    peak = jnp.max(seen_ref[...], keepdims=True)
    new = subcycle(row_ref[0], total_rows, *full, peak)
    for at in range(3):
        state_ref[at] = new[at]
    rotation = turning(row_ref[0], total_rows, depth.shape)
    row = offers(rotation, depth, wet, *new, push_x, push_y, fresh, courant / peak)
    peak_ref[...] = jnp.broadcast_to(row, peak_ref.shape)


def step_from(total_rows, row_ref, kept_ref, old, peak):
    return subcycle(
        row_ref[0], total_rows, kept_ref[0], kept_ref[1], *old, kept_ref[2], kept_ref[3], kept_ref[4], peak
    )


def middle_kernel(total_rows, row_ref, kept_ref, old_ref, rows_ref, second_ref, third_ref, peak_ref, guess_ref):
    rows = rows_ref[...]
    peak = lane_max(rows, 0)
    guess = jnp.max(offered(rows, courant / peak), keepdims=True)
    second = step_from(total_rows, row_ref, kept_ref, [old_ref[at] for at in range(3)], peak)
    third = step_from(total_rows, row_ref, kept_ref, second, guess)
    true_second = finish(kept_ref[0], kept_ref[1], second, second_ref, peak_ref)
    true_third = finish(kept_ref[0], kept_ref[1], third, third_ref, peak_ref)
    lane = lax.broadcasted_iota(jnp.int32, peak_ref.shape, 1)
    peak_ref[...] = jnp.where(lane == 0, true_second, jnp.where(lane == 1, true_third, 0.0))
    guess_ref[...] = jnp.broadcast_to(guess, guess_ref.shape)


def last_kernel(total_rows, row_ref, kept_ref, old_ref, rows_ref, guess_ref, out_ref, good_ref):
    rows = rows_ref[...]
    new = step_from(total_rows, row_ref, kept_ref, [old_ref[at] for at in range(3)], lane_max(rows, 1))
    for at in range(3):
        out_ref[at] = new[at][: out_ref.shape[1], :128]
    true = lane_max(rows, 0)
    good = jnp.abs(true - guess_ref[0:1, 0:1]) <= CLOSE * true
    good_ref[...] = jnp.broadcast_to(jnp.where(good, 1, 0), good_ref.shape)


def redo_kernel(total_rows, row_ref, kept_ref, old_ref, rows_ref, state_ref, peak_ref):
    new = step_from(total_rows, row_ref, kept_ref, [old_ref[at] for at in range(3)], lane_max(rows_ref[...], 0))
    peak = finish(kept_ref[0], kept_ref[1], new, state_ref, peak_ref)
    lane = lax.broadcasted_iota(jnp.int32, peak_ref.shape, 1)
    peak_ref[...] = jnp.where(lane == 1, peak, 0.0)


def call_small(kernel, scalars, arrays, out_shape):
    return pl.pallas_call(
        kernel, in_specs=[SMEM] * len(scalars) + [VMEM] * len(arrays), out_shape=out_shape, compiler_params=params(8)
    )(*scalars, *arrays)


def shards(
    atm_fields,
    send_cols,
    live_blocks,
    remap_weights,
    row_map,
    ocean_depth,
    wet_mask,
    sea_level,
    east_vel,
    north_vel,
):
    rows, cols = ocean_depth.shape
    total_rows = rows * axes_size(DOM)
    first_row = (lax.axis_index(DOM) * rows).reshape(1).astype(jnp.int32)
    wide = (rows + 2 * EDGE, 2 * cols)
    three = jax.ShapeDtypeStruct((3, *wide), F32)
    five = jax.ShapeDtypeStruct((5, *wide), F32)
    rim = jax.ShapeDtypeStruct((KEPT + 2, EDGE, cols), F32)
    peak_shape = jax.ShapeDtypeStruct((axes_size(PLANE), 128), F32)

    seen = exchange(first_speed(ocean_depth, wet_mask, east_vel, north_vel), DOM)
    picked = pick(atm_fields, send_cols)
    picked = insert(seen, picked)
    received = lax.all_to_all(picked, "comp", split_axis=0, concat_axis=0, tiled=True)
    fluxes, own, head, tail, seen = remap(
        live_blocks, received, remap_weights, row_map, ocean_depth, wet_mask, sea_level, east_vel, north_vel
    )
    east, west = neighbours(head, tail, ("comp",))
    top, bottom = call_small(edges_kernel, (), (own, east, west), [rim, rim])
    after, before = neighbours(top, bottom, DOM)
    kept, state, peak = call_small(
        functools.partial(first_kernel, total_rows),
        (first_row,),
        (own, east, west, after, before, seen),
        [five, three, peak_shape],
    )
    (chosen,) = call_small(
        choose_kernel, (), (exchange(peak, PLANE), seen), [jax.ShapeDtypeStruct((axes_size(COLUMN), 128), F32)]
    )
    second, third, peak, guess = call_small(
        functools.partial(middle_kernel, total_rows),
        (first_row,),
        (kept, state, exchange(chosen, COLUMN)),
        [three, three, peak_shape, jax.ShapeDtypeStruct((8, 128), F32)],
    )
    result = jax.ShapeDtypeStruct((3, rows, cols), F32)
    flag = jax.ShapeDtypeStruct((8, 128), jnp.int32)
    seen = everyone(peak)
    state, good = call_small(
        functools.partial(last_kernel, total_rows), (first_row,), (kept, third, seen, guess), [result, flag]
    )

    def again():
        state, peak = call_small(
            functools.partial(redo_kernel, total_rows), (first_row,), (kept, second, seen), [three, peak_shape]
        )
        return call_small(
            functools.partial(last_kernel, total_rows), (first_row,), (kept, state, everyone(peak), guess), [result, flag]
        )[0]

    state = lax.cond(good[0, 0] == 1, lambda: state, again)
    return fluxes, state


def solution(mesh):
    split = Mesh(mesh.devices.reshape(mesh.shape["comp"], *DOM_SHAPE), COMP_DOM)
    return jax.shard_map(
        shards,
        mesh=split,
        in_specs=(
            P(None, COMP_DOM),
            P("comp", DOM, None, None, None),
            P("comp", DOM, None),
            P("comp", DOM, None, None, None, None),
            P("comp", DOM, None, None, None),
            P(DOM, "comp"),
            P(DOM, "comp"),
            P(DOM, "comp"),
            P(DOM, "comp"),
            P(DOM, "comp"),
        ),
        out_specs=(P(None, DOM, "comp"), P(None, DOM, "comp")),
        check_vma=False,
    )
```

```python
import functools

import jax
import jax.numpy as jnp
from jax import lax
from jax.experimental import pallas as pl
from jax.experimental.pallas import tpu as pltpu
from jax.sharding import Mesh
from jax.sharding import PartitionSpec as P

DOM_SHAPE = (12, 4, 2)
COMP_DOM = ("comp", "dom_0", "dom_1", "dom_2")
DOM = ("dom_0", "dom_1", "dom_2")
PLANE = ("comp", "dom_1")
COLUMN = ("dom_0", "dom_2")
BF16 = jnp.bfloat16
F32 = jnp.float32

courant = 0.5
friction = 0.05

EDGE = 8
KEPT = 8
HIGH = 8
NT = (((1,), (1,)), ((), ()))
HBM = pl.BlockSpec(memory_space=pltpu.HBM)
SMEM = pl.BlockSpec(memory_space=pltpu.SMEM)
VMEM = pl.BlockSpec(memory_space=pltpu.VMEM)


def params(mib):
    return pltpu.CompilerParams(vmem_limit_bytes=mib * 1024 * 1024)


def axes_size(axes):
    return functools.reduce(lambda a, b: a * b, [lax.axis_size(a) for a in axes])


def neighbours(head, tail, axes):
    count = axes_size(axes)
    after = lax.ppermute(head, axes, [(i + 1, i) for i in range(count - 1)])
    before = lax.ppermute(tail, axes, [(i, i + 1) for i in range(count - 1)])
    return after, before


def fetch(refs, buffers, sems, first=0):
    copies = [pltpu.make_async_copy(ref, buf, sems.at[first + i]) for i, (ref, buf) in enumerate(zip(refs, buffers))]
    for copy in copies:
        copy.start()
    return copies


def rows16(row, count):
    tile = jnp.broadcast_to(row.astype(F32), (16, row.shape[1])).astype(BF16)
    return jnp.concatenate([tile] * (count // 16), axis=0)


def onehot(row, count):
    at = lax.broadcasted_iota(jnp.int32, (count, row.shape[1]), 0).astype(F32).astype(BF16)
    return jnp.where(at == rows16(row, count), jnp.ones_like(at), jnp.zeros_like(at))


def pick_kernel(
    fields_hbm, cols_hbm, depth_hbm, wet_hbm, east_hbm, north_hbm, out_ref, fields_ref, cols_ref, real_ref, wet_ref, sems
):
    copies = fetch(
        (fields_hbm, cols_hbm, depth_hbm, east_hbm, north_hbm, wet_hbm),
        (fields_ref, cols_ref, real_ref.at[0], real_ref.at[1], real_ref.at[2], wet_ref),
        sems,
    )
    for copy in copies:
        copy.wait()
    nfield, ncol = fields_ref.shape
    high = ncol // 256
    rows = [fields_ref[:, h * 256 : (h + 1) * 256].astype(F32) for h in range(high)]
    table = jnp.concatenate(rows, axis=0).astype(BF16)
    groups, blocks, width = cols_ref.shape[2:]
    peak = peak_of(real_ref[0], wet_ref[...].astype(F32), real_ref[1], real_ref[2])
    peak = jnp.broadcast_to(peak, (nfield, 128))
    big = peak.astype(BF16).astype(F32)
    middle = (peak - big).astype(BF16).astype(F32)
    row = lax.broadcasted_iota(jnp.int32, peak.shape, 0)
    three = jnp.where(row == 0, big, jnp.where(row == 1, middle, jnp.where(row == 2, peak - big - middle, 0.0)))
    for c in range(groups):
        for k in range(blocks):
            cols = cols_ref[0, 0, c, k : k + 1, :]
            both = jnp.dot(table, onehot(cols & 255, 256), preferred_element_type=F32)
            upper = jnp.broadcast_to(cols >> 8, (nfield, width))
            picked = both[:nfield]
            for h in range(1, high):
                picked = jnp.where(upper == h, both[h * nfield : (h + 1) * nfield], picked)
            out_ref[c, :, k * width : (k + 1) * width] = picked.astype(BF16)
        out_ref[c, :, blocks * width :] = three.astype(BF16)


def pick(fields, cols, depth, wet, east, north):
    groups, blocks, width = cols.shape[2:]
    return pl.pallas_call(
        pick_kernel,
        in_specs=[HBM] * 6,
        out_specs=VMEM,
        out_shape=jax.ShapeDtypeStruct((groups, fields.shape[0], blocks * width + 128), BF16),
        scratch_shapes=[
            pltpu.VMEM(fields.shape, BF16),
            pltpu.VMEM(cols.shape, jnp.int32),
            pltpu.VMEM((3, *depth.shape), F32),
            pltpu.VMEM(depth.shape, jnp.int32),
            pltpu.SemaphoreType.DMA((6,)),
        ],
        compiler_params=params(56),
    )(fields, cols, depth, wet, east, north)


def peak_of(depth, wet, east, north):
    return jnp.max(jnp.sqrt(depth) + wet * (jnp.abs(east) + jnp.abs(north)), keepdims=True)


def exchange(peak, axes):
    return lax.all_to_all(peak, axes, split_axis=0, concat_axis=0, tiled=True)


def everyone(peak):
    return exchange(spread_max(exchange(peak, PLANE), COLUMN), COLUMN)


def spread_max(seen, axes):
    return jnp.broadcast_to(jnp.max(seen, axis=0, keepdims=True), (axes_size(axes), 128))


def remap_kernel(
    live_ref, picked_hbm, weights_hbm, cells_hbm, depth_hbm, wet_hbm, level_hbm, east_hbm, north_hbm,
    flux_ref, own_ref, head_ref, tail_ref, peak_ref,
    picked_ref, weights_ref, cells_ref, wet_ref, spread_ref, total_ref, sems,
):
    groups, nfield, width = picked_ref.shape
    blocks = weights_ref.shape[1]
    pair_rows = 2 * nfield
    lows = total_ref.shape[1]
    first = fetch((picked_hbm, cells_hbm), (picked_ref, cells_ref), sems)
    loads = fetch([weights_hbm.at[0, 0, c] for c in range(groups)], [weights_ref.at[c] for c in range(groups)], sems, 2)
    rest = fetch(
        (depth_hbm, level_hbm, east_hbm, north_hbm, wet_hbm),
        (own_ref.at[0], own_ref.at[2], own_ref.at[3], own_ref.at[4], wet_ref),
        sems,
        2 + groups,
    )
    for copy in first:
        copy.wait()
    peak = None
    for c in range(groups):
        three = picked_ref[c, :, blocks * 256 :].astype(F32)
        one = three[0:1] + (three[1:2] + three[2:3])
        peak = one if peak is None else jnp.maximum(peak, one)
    peak_ref[...] = jnp.broadcast_to(peak, peak_ref.shape)
    for c in range(groups):
        loads[c].wait()
        live = live_ref[0, 0, c]
        onehots = []
        for k in range(blocks):
            part = slice(k * 256, (k + 1) * 256)
            contrib = lax.dot_general(picked_ref[c, :, part], weights_ref[c, k], NT, preferred_element_type=F32)
            big = contrib.astype(BF16).astype(F32)
            pair = jnp.concatenate([big, contrib - big], axis=0).astype(BF16)
            cell = cells_ref[0, 0, c, k : k + 1, :]
            upper = rows16(jnp.where(jnp.int32(k) < live, (cell >> 7) & (HIGH - 1), -1), pair_rows)
            for h in range(HIGH):
                spread_ref[h * pair_rows : (h + 1) * pair_rows, part] = jnp.where(
                    upper == BF16(h), pair, jnp.zeros_like(pair)
                )
            row, column = cell >> 7, cell & 127
            low = (row // HIGH) * 128 + column
            tiles = [onehot(jnp.where(low >> 8 == t, low & 255, -1), 256) for t in range(lows // 256)]
            onehots.append(jnp.concatenate(tiles, axis=0))
        added = lax.dot_general(
            spread_ref[...], jnp.concatenate(onehots, axis=1), NT, preferred_element_type=F32
        )
        if c == 0:
            total_ref[...] = added
        else:
            total_ref[...] += added
    for h in range(HIGH):
        base = h * pair_rows
        both = total_ref[base : base + nfield, :] + total_ref[base + nfield : base + pair_rows, :]
        for r in range(lows // 128):
            flux_ref[:, r * HIGH + h, :] = both[:, r * 128 : (r + 1) * 128]
    for copy in rest:
        copy.wait()
    own_ref[1] = wet_ref[...].astype(F32)
    own_ref[5] = flux_ref[0] / own_ref[0]
    own_ref[6] = flux_ref[1] / own_ref[0]
    own_ref[7] = flux_ref[2]
    lane = lax.broadcasted_iota(jnp.int32, head_ref.shape, 1)
    head = own_ref[0]
    tail = pltpu.roll(own_ref[0], EDGE, 1)
    for at in range(1, KEPT):
        here = lane // EDGE == at
        head = jnp.where(here, pltpu.roll(own_ref[at], at * EDGE, 1), head)
        tail = jnp.where(here, pltpu.roll(own_ref[at], (at + 1) * EDGE, 1), tail)
    head_ref[...] = head
    tail_ref[...] = tail


def remap(live, picked, weights, cells, depth, wet, level, east, north):
    groups, nfield, width = picked.shape
    rows, cols = depth.shape
    tile = jax.ShapeDtypeStruct((rows, cols), F32)
    return pl.pallas_call(
        remap_kernel,
        in_specs=[SMEM] + [HBM] * 8,
        out_specs=[VMEM] * 5,
        out_shape=[
            jax.ShapeDtypeStruct((nfield, rows, cols), F32),
            jax.ShapeDtypeStruct((KEPT, rows, cols), F32),
            tile,
            tile,
            jax.ShapeDtypeStruct((8, 128), F32),
        ],
        scratch_shapes=[
            pltpu.VMEM(picked.shape, BF16),
            pltpu.VMEM(weights.shape[2:], BF16),
            pltpu.VMEM(cells.shape, jnp.int32),
            pltpu.VMEM((rows, cols), jnp.int32),
            pltpu.VMEM((HIGH * 2 * nfield, cells.shape[3] * cells.shape[4]), BF16),
            pltpu.VMEM((HIGH * 2 * nfield, rows // HIGH * cols), F32),
            pltpu.SemaphoreType.DMA((groups + 7,)),
        ],
        compiler_params=params(56),
    )(live, picked, weights, cells, depth, wet, level, east, north)


def edges_kernel(own_ref, east_ref, west_ref, top_ref, bottom_ref):
    rows = own_ref.shape[1]
    for ref, part in ((top_ref, slice(0, EDGE)), (bottom_ref, slice(rows - EDGE, rows))):
        ref[:KEPT] = own_ref[:, part, :]
        ref[KEPT] = east_ref[part, :]
        ref[KEPT + 1] = west_ref[part, :]


def beside(at, east, west):
    lane = lax.broadcasted_iota(jnp.int32, east.shape, 1)
    return jnp.where(
        lane < 64,
        pltpu.roll(east, (128 - at * EDGE) % 128, 1),
        pltpu.roll(west, (128 - EDGE - at * EDGE) % 128, 1),
    )


def extended(at, own_ref, east_ref, west_ref, after_ref, before_ref):
    left = jnp.concatenate([own_ref[at], after_ref[at], before_ref[at]], axis=0)
    right = [beside(at, east_ref[...], west_ref[...])]
    right += [beside(at, ref[KEPT], ref[KEPT + 1]) for ref in (after_ref, before_ref)]
    return jnp.concatenate([left, jnp.concatenate(right, axis=0)], axis=1)


def turning(first_row, total_rows, shape):
    row = lax.broadcasted_iota(jnp.int32, shape, 0)
    row = first_row + jnp.where(row < shape[0] - EDGE, row, row - shape[0])
    return 0.1 + 0.4 * (row.astype(F32) + 0.5) / total_rows


def subcycle(first_row, total_rows, depth, wet, level, east, north, push_x, push_y, fresh, peak):
    step_dt = courant / peak
    rotation = turning(first_row, total_rows, depth.shape)
    flux_x = depth * east * wet
    flux_y = depth * north * wet
    diverge = 0.5 * (across(flux_x) + along(flux_y))
    level = wet * (level + step_dt * (fresh - diverge))
    grad_x = 0.5 * across(level)
    grad_y = 0.5 * along(level)
    new_east = wet * (east + step_dt * (rotation * north - grad_x + push_x - friction * east))
    new_north = wet * (north + step_dt * (-rotation * east - grad_y + push_y - friction * north))
    return level, new_east, new_north


def across(x):
    return pltpu.roll(x, x.shape[1] - 1, 1) - pltpu.roll(x, 1, 1)


def along(x):
    return pltpu.roll(x, x.shape[0] - 1, 0) - pltpu.roll(x, 1, 0)


SAMPLES = ((1.0, 0.0), (0.6, 0.0), (1.0, 0.5), (0.6, 0.25))
SLOT = 32
TERMS = 19
CLOSE = 4e-6


def curve(terms, p, q):
    def one(c):
        parts = [c[3 * a] + q * (c[3 * a + 1] + q * c[3 * a + 2]) for a in range(3)]
        return jnp.abs(parts[0] + p * (parts[1] + p * parts[2]))

    return terms[0] + one(terms[1:10]) + one(terms[10:19])


def powers(depth, wet, rotation, level, east, north, push_x=None, push_y=None, fresh=None):
    drift = -0.5 * (across(depth * east * wet) + along(depth * north * wet))
    turn_x, turn_y = rotation * north - friction * east, -rotation * east - friction * north
    if fresh is not None:
        drift, turn_x, turn_y = drift + fresh, turn_x + push_x, turn_y + push_y
    drift = wet * drift
    if level is not None:
        still = wet * level
        turn_x, turn_y = turn_x - 0.5 * across(still), turn_y - 0.5 * along(still)
    else:
        still = None
    return (
        (still, wet * east, wet * north),
        (drift, wet * turn_x, wet * turn_y),
        (None, wet * (-0.5 * across(drift)), wet * (-0.5 * along(drift))),
    )


def offers(rotation, depth, wet, level, east, north, push_x, push_y, fresh, peak):
    own = (slice(0, depth.shape[0] - 2 * EDGE), slice(0, 128))
    forcing = (push_x, push_y, fresh)
    u, v = [], []
    for a, part in enumerate(powers(depth, wet, rotation, level, east, north, *forcing)):
        for two in powers(depth, wet, rotation, *part, *(forcing if a == 0 else ())):
            u.append(two[1][own])
            v.append(two[2][own])
    terms = [jnp.sqrt(depth[own])] + u + v
    shape = terms[0].shape
    index = lax.broadcasted_iota(jnp.int32, shape, 0) * 128 + lax.broadcasted_iota(jnp.int32, shape, 1)
    lane = lax.broadcasted_iota(jnp.int32, (1, 128), 1)
    dt = courant / peak
    row = jnp.where(lane == SLOT - 1, peak, 0.0)
    for j, (p, q) in enumerate(SAMPLES):
        speed = curve(terms, p * dt, q * dt)
        fastest = speed == jnp.max(speed, keepdims=True)
        first = jnp.min(jnp.where(fastest, index, shape[0] * 128), keepdims=True)
        for i, term in enumerate(terms):
            value = jnp.sum(jnp.where(index == first, term, 0.0), keepdims=True)
            row = jnp.where(lane == SLOT * j + i, value, row)
    return row


def offered(rows, p, q):
    lane = lax.broadcasted_iota(jnp.int32, rows.shape, 1)
    terms = [rows] + [pltpu.roll(rows, 128 - i, 1) for i in range(1, TERMS)]
    return jnp.where(lane % SLOT == 0, curve(terms, p, q), 0.0)


def choose_kernel(rows_ref, out_ref):
    rows = rows_ref[...]
    count = rows.shape[0]
    lane = lax.broadcasted_iota(jnp.int32, rows.shape, 1)
    dt = courant / lane_max(rows, SLOT - 1)
    p, q = jnp.zeros(rows.shape, F32), jnp.zeros(rows.shape, F32)
    for j, (first, second) in enumerate(SAMPLES):
        p = jnp.where(lane // SLOT == j, first, p)
        q = jnp.where(lane // SLOT == j, second, q)
    speed = offered(rows, p * dt, q * dt)
    number = lax.broadcasted_iota(jnp.int32, rows.shape, 0)
    best = jnp.min(jnp.where(speed == jnp.max(speed, axis=0, keepdims=True), number, count), axis=0, keepdims=True)
    chosen = jnp.where((number == best) & (lane % SLOT == 0), 1.0, 0.0)
    for shift in (1, 2, 4, 8, 16):
        chosen = chosen + pltpu.roll(chosen, shift, 1)
    row = jnp.sum(jnp.where(chosen > 0.0, rows, 0.0), axis=0, keepdims=True)
    row = jnp.where(lane[:1] == SLOT - 1, jnp.max(rows, axis=0, keepdims=True), row)
    out_ref[...] = jnp.broadcast_to(row, out_ref.shape)


def lane_max(rows, at):
    lane = lax.broadcasted_iota(jnp.int32, rows.shape, 1)
    return jnp.max(jnp.where(lane == at, rows, 0.0), keepdims=True)


def offer_kernel(
    total_rows, row_ref, own_ref, east_ref, west_ref, after_ref, before_ref, seen_ref, kept_ref, state_ref, row_out_ref
):
    full = [extended(at, own_ref, east_ref, west_ref, after_ref, before_ref) for at in range(KEPT)]
    depth, wet, level, east, north, push_x, push_y, fresh = full
    for at, array in enumerate((depth, wet, push_x, push_y, fresh)):
        kept_ref[at] = array
    for at, array in enumerate((level, east, north)):
        state_ref[at] = array
    rotation = turning(row_ref[0], total_rows, depth.shape)
    row = offers(rotation, depth, wet, level, east, north, push_x, push_y, fresh, jnp.max(seen_ref[...], keepdims=True))
    row_out_ref[...] = jnp.broadcast_to(row, row_out_ref.shape)


def step_from(total_rows, row_ref, kept_ref, old, peak):
    return subcycle(
        row_ref[0], total_rows, kept_ref[0], kept_ref[1], *old, kept_ref[2], kept_ref[3], kept_ref[4], peak
    )


def local_peak(kept_ref, state):
    depth, wet = kept_ref[0], kept_ref[1]
    own = (slice(0, depth.shape[0] - 2 * EDGE), slice(0, 128))
    return peak_of(depth[own], wet[own], state[1][own], state[2][own])


def middle_kernel(total_rows, row_ref, kept_ref, old_ref, rows_ref, third_ref, peak_ref, guess_ref):
    rows = rows_ref[...]
    peaks = [lane_max(rows, SLOT - 1)]
    peaks.append(jnp.max(offered(rows, courant / peaks[0], 0.0), keepdims=True))
    peaks.append(jnp.max(offered(rows, courant / peaks[0], courant / peaks[1]), keepdims=True))
    state = [old_ref[at] for at in range(3)]
    lane = lax.broadcasted_iota(jnp.int32, (1, 128), 1)
    row = jnp.zeros((1, 128), F32)
    for at in range(3):
        state = step_from(total_rows, row_ref, kept_ref, state, peaks[at])
        row = jnp.where(lane == at, local_peak(kept_ref, state), row)
    for at in range(3):
        third_ref[at] = state[at]
    peak_ref[...] = jnp.broadcast_to(row, peak_ref.shape)
    guess_ref[...] = jnp.broadcast_to(jnp.where(lane == 0, peaks[1], peaks[2]), guess_ref.shape)


def last_kernel(total_rows, row_ref, kept_ref, old_ref, rows_ref, guess_ref, out_ref, good_ref):
    rows = rows_ref[...]
    new = step_from(total_rows, row_ref, kept_ref, [old_ref[at] for at in range(3)], lane_max(rows, 2))
    for at in range(3):
        out_ref[at] = new[at][: out_ref.shape[1], :128]
    lane = lax.broadcasted_iota(jnp.int32, (1, 128), 1)
    true = jnp.max(rows, axis=0, keepdims=True)
    off = jnp.where(lane < 2, jnp.abs(true - guess_ref[0:1, :]) - CLOSE * true, -1.0)
    good_ref[...] = jnp.broadcast_to(jnp.where(jnp.max(off, keepdims=True) <= 0.0, 1, 0), good_ref.shape)


def redo_kernel(total_rows, at, row_ref, kept_ref, old_ref, rows_ref, state_ref, peak_ref):
    new = step_from(total_rows, row_ref, kept_ref, [old_ref[i] for i in range(3)], lane_max(rows_ref[...], at))
    for i in range(3):
        state_ref[i] = new[i]
    peak_ref[...] = jnp.broadcast_to(local_peak(kept_ref, new), peak_ref.shape)


def call_small(kernel, scalars, arrays, out_shape):
    return pl.pallas_call(
        kernel, in_specs=[SMEM] * len(scalars) + [VMEM] * len(arrays), out_shape=out_shape, compiler_params=params(8)
    )(*scalars, *arrays)


def shards(
    atm_fields,
    send_cols,
    live_blocks,
    remap_weights,
    row_map,
    ocean_depth,
    wet_mask,
    sea_level,
    east_vel,
    north_vel,
):
    rows, cols = ocean_depth.shape
    total_rows = rows * axes_size(DOM)
    first_row = (lax.axis_index(DOM) * rows).reshape(1).astype(jnp.int32)
    wide = (rows + 2 * EDGE, 2 * cols)
    three = jax.ShapeDtypeStruct((3, *wide), F32)
    five = jax.ShapeDtypeStruct((5, *wide), F32)
    rim = jax.ShapeDtypeStruct((KEPT + 2, EDGE, cols), F32)
    peak_shape = jax.ShapeDtypeStruct((axes_size(PLANE), 128), F32)

    picked = pick(atm_fields, send_cols, ocean_depth, wet_mask, east_vel, north_vel)
    received = lax.all_to_all(picked, "comp", split_axis=0, concat_axis=0, tiled=True)
    fluxes, own, head, tail, seen = remap(
        live_blocks, received, remap_weights, row_map, ocean_depth, wet_mask, sea_level, east_vel, north_vel
    )
    east, west = neighbours(head, tail, ("comp",))
    top, bottom = call_small(edges_kernel, (), (own, east, west), [rim, rim])
    after, before = neighbours(top, bottom, DOM)
    kept, start, row = call_small(
        functools.partial(offer_kernel, total_rows),
        (first_row,),
        (own, east, west, after, before, seen),
        [five, three, peak_shape],
    )
    (row,) = call_small(
        choose_kernel, (), (exchange(row, PLANE),), [jax.ShapeDtypeStruct((axes_size(COLUMN), 128), F32)]
    )
    first = exchange(row, COLUMN)
    third, peak, guess = call_small(
        functools.partial(middle_kernel, total_rows),
        (first_row,),
        (kept, start, first),
        [three, peak_shape, jax.ShapeDtypeStruct((8, 128), F32)],
    )

    def last(third, seen):
        return call_small(
            functools.partial(last_kernel, total_rows),
            (first_row,),
            (kept, third, seen, guess),
            [jax.ShapeDtypeStruct((3, rows, cols), F32), jax.ShapeDtypeStruct((8, 128), jnp.int32)],
        )

    state, good = last(third, everyone(peak))

    def again():
        state, seen, at = start, first, SLOT - 1
        for _ in range(3):
            state, peak = call_small(
                functools.partial(redo_kernel, total_rows, at), (first_row,), (kept, state, seen), [three, peak_shape]
            )
            seen, at = everyone(peak), 2
        return last(state, seen)[0]

    state = lax.cond(good[0, 0] == 1, lambda: state, again)
    return fluxes, state


def solution(mesh):
    split = Mesh(mesh.devices.reshape(mesh.shape["comp"], *DOM_SHAPE), COMP_DOM)
    return jax.shard_map(
        shards,
        mesh=split,
        in_specs=(
            P(None, COMP_DOM),
            P("comp", DOM, None, None, None),
            P("comp", DOM, None),
            P("comp", DOM, None, None, None, None),
            P("comp", DOM, None, None, None),
            P(DOM, "comp"),
            P(DOM, "comp"),
            P(DOM, "comp"),
            P(DOM, "comp"),
            P(DOM, "comp"),
        ),
        out_specs=(P(None, DOM, "comp"), P(None, DOM, "comp")),
        check_vma=False,
    )
```

```python
import functools

import jax
import jax.numpy as jnp
from jax import lax
from jax.experimental import pallas as pl
from jax.experimental.pallas import tpu as pltpu
from jax.sharding import Mesh
from jax.sharding import PartitionSpec as P

DOM_SHAPE = (12, 4, 2)
COMP_DOM = ("comp", "dom_0", "dom_1", "dom_2")
DOM = ("dom_0", "dom_1", "dom_2")
PLANE = ("comp", "dom_1")
COLUMN = ("dom_0", "dom_2")
BF16 = jnp.bfloat16
F32 = jnp.float32

courant = 0.5
friction = 0.05

EDGE = 8
KEPT = 8
HIGH = 8
NT = (((1,), (1,)), ((), ()))
HBM = pl.BlockSpec(memory_space=pltpu.HBM)
SMEM = pl.BlockSpec(memory_space=pltpu.SMEM)
VMEM = pl.BlockSpec(memory_space=pltpu.VMEM)


def params(mib):
    return pltpu.CompilerParams(vmem_limit_bytes=mib * 1024 * 1024)


def axes_size(axes):
    return functools.reduce(lambda a, b: a * b, [lax.axis_size(a) for a in axes])


def neighbours(head, tail, axes):
    count = axes_size(axes)
    after = lax.ppermute(head, axes, [(i + 1, i) for i in range(count - 1)])
    before = lax.ppermute(tail, axes, [(i, i + 1) for i in range(count - 1)])
    return after, before


def fetch(refs, buffers, sems, first=0):
    copies = [pltpu.make_async_copy(ref, buf, sems.at[first + i]) for i, (ref, buf) in enumerate(zip(refs, buffers))]
    for copy in copies:
        copy.start()
    return copies


def rows16(row, count):
    tile = jnp.broadcast_to(row.astype(F32), (16, row.shape[1])).astype(BF16)
    return jnp.concatenate([tile] * (count // 16), axis=0)


def onehot(row, count):
    at = lax.broadcasted_iota(jnp.int32, (count, row.shape[1]), 0).astype(F32).astype(BF16)
    return jnp.where(at == rows16(row, count), jnp.ones_like(at), jnp.zeros_like(at))


def pick_kernel(fields_hbm, cols_hbm, out_ref, fields_ref, cols_ref, sems):
    for copy in fetch((fields_hbm, cols_hbm), (fields_ref, cols_ref), sems):
        copy.wait()
    nfield, ncol = fields_ref.shape
    high = ncol // 256
    rows = [fields_ref[:, h * 256 : (h + 1) * 256].astype(F32) for h in range(high)]
    table = jnp.concatenate(rows, axis=0).astype(BF16)
    groups, blocks, width = cols_ref.shape[2:]
    for c in range(groups):
        for k in range(blocks):
            cols = cols_ref[0, 0, c, k : k + 1, :]
            both = jnp.dot(table, onehot(cols & 255, 256), preferred_element_type=F32)
            upper = jnp.broadcast_to(cols >> 8, (nfield, width))
            picked = both[:nfield]
            for h in range(1, high):
                picked = jnp.where(upper == h, both[h * nfield : (h + 1) * nfield], picked)
            out_ref[c, :, k * width : (k + 1) * width] = picked.astype(BF16)


def pick(fields, cols):
    groups, blocks, width = cols.shape[2:]
    return pl.pallas_call(
        pick_kernel,
        in_specs=[HBM] * 2,
        out_specs=VMEM,
        out_shape=jax.ShapeDtypeStruct((groups, fields.shape[0], blocks * width), BF16),
        scratch_shapes=[
            pltpu.VMEM(fields.shape, BF16),
            pltpu.VMEM(cols.shape, jnp.int32),
            pltpu.SemaphoreType.DMA((2,)),
        ],
        compiler_params=params(56),
    )(fields, cols)


def peak_of(depth, wet, east, north):
    return jnp.max(jnp.sqrt(depth) + wet * (jnp.abs(east) + jnp.abs(north)), keepdims=True)


def exchange(peak, axes):
    return lax.all_to_all(peak, axes, split_axis=0, concat_axis=0, tiled=True)


def remap_kernel(
    live_ref, picked_hbm, weights_hbm, cells_hbm, depth_hbm, wet_hbm, level_hbm, east_hbm, north_hbm,
    flux_ref, own_ref, head_ref, tail_ref,
    picked_ref, weights_ref, cells_ref, wet_ref, spread_ref, total_ref, sems,
):
    groups, nfield, width = picked_ref.shape
    blocks = weights_ref.shape[1]
    pair_rows = 2 * nfield
    lows = total_ref.shape[1]
    first = fetch((picked_hbm, cells_hbm), (picked_ref, cells_ref), sems)
    loads = fetch([weights_hbm.at[0, 0, c] for c in range(groups)], [weights_ref.at[c] for c in range(groups)], sems, 2)
    rest = fetch(
        (depth_hbm, level_hbm, east_hbm, north_hbm, wet_hbm),
        (own_ref.at[0], own_ref.at[2], own_ref.at[3], own_ref.at[4], wet_ref),
        sems,
        2 + groups,
    )
    for copy in first:
        copy.wait()
    for c in range(groups):
        loads[c].wait()
        live = live_ref[0, 0, c]
        onehots = []
        for k in range(blocks):
            part = slice(k * 256, (k + 1) * 256)
            contrib = lax.dot_general(picked_ref[c, :, part], weights_ref[c, k], NT, preferred_element_type=F32)
            big = contrib.astype(BF16).astype(F32)
            pair = jnp.concatenate([big, contrib - big], axis=0).astype(BF16)
            cell = cells_ref[0, 0, c, k : k + 1, :]
            upper = rows16(jnp.where(jnp.int32(k) < live, (cell >> 7) & (HIGH - 1), -1), pair_rows)
            for h in range(HIGH):
                spread_ref[h * pair_rows : (h + 1) * pair_rows, part] = jnp.where(
                    upper == BF16(h), pair, jnp.zeros_like(pair)
                )
            row, column = cell >> 7, cell & 127
            low = (row // HIGH) * 128 + column
            tiles = [onehot(jnp.where(low >> 8 == t, low & 255, -1), 256) for t in range(lows // 256)]
            onehots.append(jnp.concatenate(tiles, axis=0))
        added = lax.dot_general(
            spread_ref[...], jnp.concatenate(onehots, axis=1), NT, preferred_element_type=F32
        )
        if c == 0:
            total_ref[...] = added
        else:
            total_ref[...] += added
    for h in range(HIGH):
        base = h * pair_rows
        both = total_ref[base : base + nfield, :] + total_ref[base + nfield : base + pair_rows, :]
        for r in range(lows // 128):
            flux_ref[:, r * HIGH + h, :] = both[:, r * 128 : (r + 1) * 128]
    for copy in rest:
        copy.wait()
    own_ref[1] = wet_ref[...].astype(F32)
    own_ref[5] = flux_ref[0] / own_ref[0]
    own_ref[6] = flux_ref[1] / own_ref[0]
    own_ref[7] = flux_ref[2]
    lane = lax.broadcasted_iota(jnp.int32, head_ref.shape, 1)
    head = own_ref[0]
    tail = pltpu.roll(own_ref[0], EDGE, 1)
    for at in range(1, KEPT):
        here = lane // EDGE == at
        head = jnp.where(here, pltpu.roll(own_ref[at], at * EDGE, 1), head)
        tail = jnp.where(here, pltpu.roll(own_ref[at], (at + 1) * EDGE, 1), tail)
    head_ref[...] = head
    tail_ref[...] = tail


def remap(live, picked, weights, cells, depth, wet, level, east, north):
    groups, nfield, width = picked.shape
    rows, cols = depth.shape
    tile = jax.ShapeDtypeStruct((rows, cols), F32)
    return pl.pallas_call(
        remap_kernel,
        in_specs=[SMEM] + [HBM] * 8,
        out_specs=[VMEM] * 4,
        out_shape=[
            jax.ShapeDtypeStruct((nfield, rows, cols), F32),
            jax.ShapeDtypeStruct((KEPT, rows, cols), F32),
            tile,
            tile,
        ],
        scratch_shapes=[
            pltpu.VMEM(picked.shape, BF16),
            pltpu.VMEM(weights.shape[2:], BF16),
            pltpu.VMEM(cells.shape, jnp.int32),
            pltpu.VMEM((rows, cols), jnp.int32),
            pltpu.VMEM((HIGH * 2 * nfield, cells.shape[3] * cells.shape[4]), BF16),
            pltpu.VMEM((HIGH * 2 * nfield, rows // HIGH * cols), F32),
            pltpu.SemaphoreType.DMA((groups + 7,)),
        ],
        compiler_params=params(56),
    )(live, picked, weights, cells, depth, wet, level, east, north)


def edges_kernel(own_ref, east_ref, west_ref, top_ref, bottom_ref):
    rows = own_ref.shape[1]
    for ref, part in ((top_ref, slice(0, EDGE)), (bottom_ref, slice(rows - EDGE, rows))):
        ref[:KEPT] = own_ref[:, part, :]
        ref[KEPT] = east_ref[part, :]
        ref[KEPT + 1] = west_ref[part, :]


def beside(at, east, west):
    lane = lax.broadcasted_iota(jnp.int32, east.shape, 1)
    return jnp.where(
        lane < 64,
        pltpu.roll(east, (128 - at * EDGE) % 128, 1),
        pltpu.roll(west, (128 - EDGE - at * EDGE) % 128, 1),
    )


def extended(at, own_ref, east_ref, west_ref, after_ref, before_ref):
    left = jnp.concatenate([own_ref[at], after_ref[at], before_ref[at]], axis=0)
    right = [beside(at, east_ref[...], west_ref[...])]
    right += [beside(at, ref[KEPT], ref[KEPT + 1]) for ref in (after_ref, before_ref)]
    return jnp.concatenate([left, jnp.concatenate(right, axis=0)], axis=1)


def turning(first_row, total_rows, shape):
    row = lax.broadcasted_iota(jnp.int32, shape, 0)
    row = first_row + jnp.where(row < shape[0] - EDGE, row, row - shape[0])
    return 0.1 + 0.4 * (row.astype(F32) + 0.5) / total_rows


def subcycle(first_row, total_rows, depth, wet, level, east, north, push_x, push_y, fresh, peak):
    step_dt = courant / peak
    rotation = turning(first_row, total_rows, depth.shape)
    flux_x = depth * east * wet
    flux_y = depth * north * wet
    diverge = 0.5 * (across(flux_x) + along(flux_y))
    level = wet * (level + step_dt * (fresh - diverge))
    grad_x = 0.5 * across(level)
    grad_y = 0.5 * along(level)
    new_east = wet * (east + step_dt * (rotation * north - grad_x + push_x - friction * east))
    new_north = wet * (north + step_dt * (-rotation * east - grad_y + push_y - friction * north))
    return level, new_east, new_north


def across(x):
    return pltpu.roll(x, x.shape[1] - 1, 1) - pltpu.roll(x, 1, 1)


def along(x):
    return pltpu.roll(x, x.shape[0] - 1, 0) - pltpu.roll(x, 1, 0)


SAMPLES = ((0.5, 0.0), (0.25, 0.0), (0.5, 0.25), (0.25, 0.12))
SLOT = 32
TERMS = 19
CLOSE = 4e-6


def curve(terms, p, q):
    def one(c):
        parts = [c[3 * a] + q * (c[3 * a + 1] + q * c[3 * a + 2]) for a in range(3)]
        return jnp.abs(parts[0] + p * (parts[1] + p * parts[2]))

    return terms[0] + one(terms[1:10]) + one(terms[10:19])


def powers(depth, wet, rotation, level, east, north, push_x=None, push_y=None, fresh=None):
    drift = -0.5 * (across(depth * east * wet) + along(depth * north * wet))
    turn_x, turn_y = rotation * north - friction * east, -rotation * east - friction * north
    if fresh is not None:
        drift, turn_x, turn_y = drift + fresh, turn_x + push_x, turn_y + push_y
    drift = wet * drift
    if level is not None:
        still = wet * level
        turn_x, turn_y = turn_x - 0.5 * across(still), turn_y - 0.5 * along(still)
    else:
        still = None
    return (
        (still, wet * east, wet * north),
        (drift, wet * turn_x, wet * turn_y),
        (None, wet * (-0.5 * across(drift)), wet * (-0.5 * along(drift))),
    )


def offers(rotation, depth, wet, level, east, north, push_x, push_y, fresh):
    own = (slice(0, depth.shape[0] - 2 * EDGE), slice(0, 128))
    forcing = (push_x, push_y, fresh)
    u, v = [], []
    for a, part in enumerate(powers(depth, wet, rotation, level, east, north, *forcing)):
        for two in powers(depth, wet, rotation, *part, *(forcing if a == 0 else ())):
            u.append(two[1][own])
            v.append(two[2][own])
    terms = [jnp.sqrt(depth[own])] + u + v
    shape = terms[0].shape
    index = lax.broadcasted_iota(jnp.int32, shape, 0) * 128 + lax.broadcasted_iota(jnp.int32, shape, 1)
    lane = lax.broadcasted_iota(jnp.int32, (1, 128), 1)
    peak = peak_of(depth[own], wet[own], east[own], north[own])
    dt = courant / peak
    row = jnp.where(lane == SLOT - 1, peak, 0.0)
    for j, (p, q) in enumerate(SAMPLES):
        speed = curve(terms, p * dt, q * dt)
        fastest = speed == jnp.max(speed, keepdims=True)
        first = jnp.min(jnp.where(fastest, index, shape[0] * 128), keepdims=True)
        for i, term in enumerate(terms):
            value = jnp.sum(jnp.where(index == first, term, 0.0), keepdims=True)
            row = jnp.where(lane == SLOT * j + i, value, row)
    return row


def offered(rows, p, q):
    lane = lax.broadcasted_iota(jnp.int32, rows.shape, 1)
    terms = [rows] + [pltpu.roll(rows, 128 - i, 1) for i in range(1, TERMS)]
    return jnp.where(lane % SLOT == 0, curve(terms, p, q), 0.0)


def choose_kernel(rows_ref, out_ref):
    rows = rows_ref[...]
    count = rows.shape[0]
    lane = lax.broadcasted_iota(jnp.int32, rows.shape, 1)
    dt = courant / lane_max(rows, SLOT - 1)
    p, q = jnp.zeros(rows.shape, F32), jnp.zeros(rows.shape, F32)
    for j, (first, second) in enumerate(SAMPLES):
        p = jnp.where(lane // SLOT == j, first, p)
        q = jnp.where(lane // SLOT == j, second, q)
    speed = offered(rows, p * dt, q * dt)
    number = lax.broadcasted_iota(jnp.int32, rows.shape, 0)
    best = jnp.min(jnp.where(speed == jnp.max(speed, axis=0, keepdims=True), number, count), axis=0, keepdims=True)
    chosen = jnp.where((number == best) & (lane % SLOT == 0), 1.0, 0.0)
    for shift in (1, 2, 4, 8, 16):
        chosen = chosen + pltpu.roll(chosen, shift, 1)
    row = jnp.sum(jnp.where(chosen > 0.0, rows, 0.0), axis=0, keepdims=True)
    row = jnp.where(lane[:1] == SLOT - 1, jnp.max(rows, axis=0, keepdims=True), row)
    out_ref[...] = jnp.broadcast_to(row, out_ref.shape)


def lane_max(rows, at):
    lane = lax.broadcasted_iota(jnp.int32, rows.shape, 1)
    return jnp.max(jnp.where(lane == at, rows, 0.0), keepdims=True)


def offer_kernel(
    total_rows, row_ref, own_ref, east_ref, west_ref, after_ref, before_ref, kept_ref, state_ref, row_out_ref
):
    full = [extended(at, own_ref, east_ref, west_ref, after_ref, before_ref) for at in range(KEPT)]
    depth, wet, level, east, north, push_x, push_y, fresh = full
    for at, array in enumerate((depth, wet, push_x, push_y, fresh)):
        kept_ref[at] = array
    for at, array in enumerate((level, east, north)):
        state_ref[at] = array
    rotation = turning(row_ref[0], total_rows, depth.shape)
    row = offers(rotation, depth, wet, level, east, north, push_x, push_y, fresh)
    row_out_ref[...] = jnp.broadcast_to(row, row_out_ref.shape)


def most_kernel(rows_ref, out_ref):
    out_ref[...] = jnp.broadcast_to(jnp.max(rows_ref[...], axis=0, keepdims=True), out_ref.shape)


def everyone(peak):
    row = jax.ShapeDtypeStruct((axes_size(COLUMN), 128), F32)
    return exchange(call_small(most_kernel, (), (exchange(peak, PLANE),), row), COLUMN)


def step_from(total_rows, row_ref, kept_ref, old, peak):
    return subcycle(
        row_ref[0], total_rows, kept_ref[0], kept_ref[1], *old, kept_ref[2], kept_ref[3], kept_ref[4], peak
    )


def local_peak(kept_ref, state):
    depth, wet = kept_ref[0], kept_ref[1]
    own = (slice(0, depth.shape[0] - 2 * EDGE), slice(0, 128))
    return peak_of(depth[own], wet[own], state[1][own], state[2][own])


def middle_kernel(total_rows, row_ref, kept_ref, old_ref, rows_ref, third_ref, peak_ref, guess_ref):
    rows = rows_ref[...]
    peaks = [lane_max(rows, SLOT - 1)]
    peaks.append(jnp.max(offered(rows, courant / peaks[0], 0.0), keepdims=True))
    peaks.append(jnp.max(offered(rows, courant / peaks[0], courant / peaks[1]), keepdims=True))
    state = [old_ref[at] for at in range(3)]
    lane = lax.broadcasted_iota(jnp.int32, (1, 128), 1)
    row = jnp.zeros((1, 128), F32)
    for at in range(3):
        state = step_from(total_rows, row_ref, kept_ref, state, peaks[at])
        row = jnp.where(lane == at, local_peak(kept_ref, state), row)
    for at in range(3):
        third_ref[at] = state[at]
    peak_ref[...] = jnp.broadcast_to(row, peak_ref.shape)
    guess_ref[...] = jnp.broadcast_to(jnp.where(lane == 0, peaks[1], peaks[2]), guess_ref.shape)


def last_kernel(total_rows, row_ref, kept_ref, old_ref, rows_ref, guess_ref, out_ref, good_ref):
    rows = rows_ref[...]
    new = step_from(total_rows, row_ref, kept_ref, [old_ref[at] for at in range(3)], lane_max(rows, 2))
    for at in range(3):
        out_ref[at] = new[at][: out_ref.shape[1], :128]
    lane = lax.broadcasted_iota(jnp.int32, (1, 128), 1)
    true = jnp.max(rows, axis=0, keepdims=True)
    off = jnp.where(lane < 2, jnp.abs(true - guess_ref[0:1, :]) - CLOSE * true, -1.0)
    good_ref[0] = jnp.where(jnp.max(off) <= 0.0, 1, 0)


def redo_kernel(total_rows, at, row_ref, kept_ref, old_ref, rows_ref, state_ref, peak_ref):
    new = step_from(total_rows, row_ref, kept_ref, [old_ref[i] for i in range(3)], lane_max(rows_ref[...], at))
    for i in range(3):
        state_ref[i] = new[i]
    peak_ref[...] = jnp.broadcast_to(local_peak(kept_ref, new), peak_ref.shape)


def call_small(kernel, scalars, arrays, out_shape, out_specs=None):
    return pl.pallas_call(
        kernel,
        in_specs=[SMEM] * len(scalars) + [VMEM] * len(arrays),
        out_shape=out_shape,
        out_specs=jax.tree.map(lambda _: VMEM, out_shape) if out_specs is None else out_specs,
        compiler_params=params(8),
    )(*scalars, *arrays)


def shards(
    atm_fields,
    send_cols,
    live_blocks,
    remap_weights,
    row_map,
    ocean_depth,
    wet_mask,
    sea_level,
    east_vel,
    north_vel,
):
    rows, cols = ocean_depth.shape
    total_rows = rows * axes_size(DOM)
    first_row = (lax.axis_index(DOM) * rows).reshape(1).astype(jnp.int32)
    wide = (rows + 2 * EDGE, 2 * cols)
    three = jax.ShapeDtypeStruct((3, *wide), F32)
    five = jax.ShapeDtypeStruct((5, *wide), F32)
    rim = jax.ShapeDtypeStruct((KEPT + 2, EDGE, cols), F32)
    peak_shape = jax.ShapeDtypeStruct((axes_size(PLANE), 128), F32)

    picked = pick(atm_fields, send_cols)
    received = lax.all_to_all(picked, "comp", split_axis=0, concat_axis=0, tiled=True)
    fluxes, own, head, tail = remap(
        live_blocks, received, remap_weights, row_map, ocean_depth, wet_mask, sea_level, east_vel, north_vel
    )
    east, west = neighbours(head, tail, ("comp",))
    top, bottom = call_small(edges_kernel, (), (own, east, west), [rim, rim])
    after, before = neighbours(top, bottom, DOM)
    kept, start, row = call_small(
        functools.partial(offer_kernel, total_rows),
        (first_row,),
        (own, east, west, after, before),
        [five, three, peak_shape],
    )
    (row,) = call_small(
        choose_kernel, (), (exchange(row, PLANE),), [jax.ShapeDtypeStruct((axes_size(COLUMN), 128), F32)]
    )
    first = exchange(row, COLUMN)
    third, peak, guess = call_small(
        functools.partial(middle_kernel, total_rows),
        (first_row,),
        (kept, start, first),
        [three, peak_shape, jax.ShapeDtypeStruct((8, 128), F32)],
    )

    def last(third, seen):
        return call_small(
            functools.partial(last_kernel, total_rows),
            (first_row,),
            (kept, third, seen, guess),
            [jax.ShapeDtypeStruct((3, rows, cols), F32), jax.ShapeDtypeStruct((1,), jnp.int32)],
            [VMEM, SMEM],
        )

    state, good = last(third, everyone(peak))

    def again():
        state, seen, at = start, first, SLOT - 1
        for _ in range(3):
            state, peak = call_small(
                functools.partial(redo_kernel, total_rows, at), (first_row,), (kept, state, seen), [three, peak_shape]
            )
            seen, at = everyone(peak), 2
        return last(state, seen)[0]

    state = lax.cond(good[0] == 1, lambda: state, again)
    return fluxes, state


def solution(mesh):
    split = Mesh(mesh.devices.reshape(mesh.shape["comp"], *DOM_SHAPE), COMP_DOM)
    return jax.shard_map(
        shards,
        mesh=split,
        in_specs=(
            P(None, COMP_DOM),
            P("comp", DOM, None, None, None),
            P("comp", DOM, None),
            P("comp", DOM, None, None, None, None),
            P("comp", DOM, None, None, None),
            P(DOM, "comp"),
            P(DOM, "comp"),
            P(DOM, "comp"),
            P(DOM, "comp"),
            P(DOM, "comp"),
        ),
        out_specs=(P(None, DOM, "comp"), P(None, DOM, "comp")),
        check_vma=False,
    )
```

```python
import functools

import jax
import jax.numpy as jnp
from jax import lax
from jax.experimental import pallas as pl
from jax.experimental.pallas import tpu as pltpu
from jax.sharding import Mesh
from jax.sharding import PartitionSpec as P

DOM_SHAPE = (12, 4, 2)
COMP_DOM = ("comp", "dom_0", "dom_1", "dom_2")
DOM = ("dom_0", "dom_1", "dom_2")
PLANE = ("comp", "dom_1")
COLUMN = ("dom_0", "dom_2")
BF16 = jnp.bfloat16
F32 = jnp.float32

courant = 0.5
friction = 0.05

EDGE = 8
KEPT = 8
HIGH = 8
NT = (((1,), (1,)), ((), ()))
HBM = pl.BlockSpec(memory_space=pltpu.HBM)
SMEM = pl.BlockSpec(memory_space=pltpu.SMEM)
VMEM = pl.BlockSpec(memory_space=pltpu.VMEM)


def params(mib):
    return pltpu.CompilerParams(vmem_limit_bytes=mib * 1024 * 1024)


def axes_size(axes):
    return functools.reduce(lambda a, b: a * b, [lax.axis_size(a) for a in axes])


def neighbours(head, tail, axes):
    count = axes_size(axes)
    after = lax.ppermute(head, axes, [(i + 1, i) for i in range(count - 1)])
    before = lax.ppermute(tail, axes, [(i, i + 1) for i in range(count - 1)])
    return after, before


def fetch(refs, buffers, sems, first=0):
    copies = [pltpu.make_async_copy(ref, buf, sems.at[first + i]) for i, (ref, buf) in enumerate(zip(refs, buffers))]
    for copy in copies:
        copy.start()
    return copies


def rows16(row, count):
    tile = jnp.broadcast_to(row.astype(F32), (16, row.shape[1])).astype(BF16)
    return jnp.concatenate([tile] * (count // 16), axis=0)


def onehot(row, count):
    at = lax.broadcasted_iota(jnp.int32, (count, row.shape[1]), 0).astype(F32).astype(BF16)
    return jnp.where(at == rows16(row, count), jnp.ones_like(at), jnp.zeros_like(at))


def pick_kernel(fields_hbm, cols_hbm, out_ref, fields_ref, cols_ref, sems):
    for copy in fetch((fields_hbm, cols_hbm), (fields_ref, cols_ref), sems):
        copy.wait()
    nfield, ncol = fields_ref.shape
    high = ncol // 256
    rows = [fields_ref[:, h * 256 : (h + 1) * 256].astype(F32) for h in range(high)]
    table = jnp.concatenate(rows, axis=0).astype(BF16)
    groups, blocks, width = cols_ref.shape[2:]
    for c in range(groups):
        for k in range(blocks):
            cols = cols_ref[0, 0, c, k : k + 1, :]
            both = jnp.dot(table, onehot(cols & 255, 256), preferred_element_type=F32)
            upper = jnp.broadcast_to(cols >> 8, (nfield, width))
            picked = both[:nfield]
            for h in range(1, high):
                picked = jnp.where(upper == h, both[h * nfield : (h + 1) * nfield], picked)
            out_ref[c, :, k * width : (k + 1) * width] = picked.astype(BF16)


def pick(fields, cols):
    groups, blocks, width = cols.shape[2:]
    return pl.pallas_call(
        pick_kernel,
        in_specs=[HBM] * 2,
        out_specs=VMEM,
        out_shape=jax.ShapeDtypeStruct((groups, fields.shape[0], blocks * width), BF16),
        scratch_shapes=[
            pltpu.VMEM(fields.shape, BF16),
            pltpu.VMEM(cols.shape, jnp.int32),
            pltpu.SemaphoreType.DMA((2,)),
        ],
        compiler_params=params(56),
    )(fields, cols)


def peak_of(depth, wet, east, north):
    return jnp.max(jnp.sqrt(depth) + wet * (jnp.abs(east) + jnp.abs(north)), keepdims=True)


def exchange(peak, axes):
    return lax.all_to_all(peak, axes, split_axis=0, concat_axis=0, tiled=True)


FORCED = 8


def accumulate(fields, live_ref, picked_ref, weights_ref, cells_ref, spread_ref, total_ref, loads):
    groups = picked_ref.shape[0]
    blocks = weights_ref.shape[1]
    pair_rows = 2 * (fields.stop - fields.start)
    lows = total_ref.shape[1]
    for c in range(groups):
        loads[c].wait()
        live = live_ref[0, 0, c]
        onehots = []
        for k in range(blocks):
            part = slice(k * 256, (k + 1) * 256)
            contrib = lax.dot_general(picked_ref[c, :, part], weights_ref[c, k], NT, preferred_element_type=F32)
            contrib = contrib[fields]
            big = contrib.astype(BF16).astype(F32)
            pair = jnp.concatenate([big, contrib - big], axis=0).astype(BF16)
            cell = cells_ref[0, 0, c, k : k + 1, :]
            upper = rows16(jnp.where(jnp.int32(k) < live, (cell >> 7) & (HIGH - 1), -1), pair_rows)
            for h in range(HIGH):
                spread_ref[h * pair_rows : (h + 1) * pair_rows, part] = jnp.where(
                    upper == BF16(h), pair, jnp.zeros_like(pair)
                )
            row, column = cell >> 7, cell & 127
            low = (row // HIGH) * 128 + column
            tiles = [onehot(jnp.where(low >> 8 == t, low & 255, -1), 256) for t in range(lows // 256)]
            onehots.append(jnp.concatenate(tiles, axis=0))
        added = lax.dot_general(
            spread_ref[...], jnp.concatenate(onehots, axis=1), NT, preferred_element_type=F32
        )
        if c == 0:
            total_ref[...] = added
        else:
            total_ref[...] += added


def lay_out(total_ref, part_ref):
    count = part_ref.shape[0]
    for h in range(HIGH):
        base = h * 2 * count
        both = total_ref[base : base + count, :] + total_ref[base + count : base + 2 * count, :]
        for r in range(total_ref.shape[1] // 128):
            part_ref[:, r * HIGH + h, :] = both[:, r * 128 : (r + 1) * 128]


def load_blocks(picked_hbm, cells_hbm, weights_hbm, picked_ref, cells_ref, weights_ref, sems):
    groups = picked_ref.shape[0]
    first = fetch((picked_hbm, cells_hbm), (picked_ref, cells_ref), sems)
    loads = fetch([weights_hbm.at[0, 0, c] for c in range(groups)], [weights_ref.at[c] for c in range(groups)], sems, 2)
    return first, loads


def forced_kernel(
    live_ref, picked_hbm, weights_hbm, cells_hbm, depth_hbm, wet_hbm, level_hbm, east_hbm, north_hbm,
    flux_hbm, own_ref, head_ref, tail_ref,
    picked_ref, weights_ref, cells_ref, wet_ref, part_ref, spread_ref, total_ref, sems,
):
    groups = picked_ref.shape[0]
    first, loads = load_blocks(picked_hbm, cells_hbm, weights_hbm, picked_ref, cells_ref, weights_ref, sems)
    rest = fetch(
        (depth_hbm, level_hbm, east_hbm, north_hbm, wet_hbm),
        (own_ref.at[0], own_ref.at[2], own_ref.at[3], own_ref.at[4], wet_ref),
        sems,
        2 + groups,
    )
    for copy in first:
        copy.wait()
    accumulate(slice(0, FORCED), live_ref, picked_ref, weights_ref, cells_ref, spread_ref, total_ref, loads)
    lay_out(total_ref, part_ref)
    store = pltpu.make_async_copy(part_ref, flux_hbm.at[pl.ds(0, FORCED)], sems.at[7 + groups])
    store.start()
    for copy in rest:
        copy.wait()
    own_ref[1] = wet_ref[...].astype(F32)
    own_ref[5] = part_ref[0] / own_ref[0]
    own_ref[6] = part_ref[1] / own_ref[0]
    own_ref[7] = part_ref[2]
    lane = lax.broadcasted_iota(jnp.int32, head_ref.shape, 1)
    head = own_ref[0]
    tail = pltpu.roll(own_ref[0], EDGE, 1)
    for at in range(1, KEPT):
        here = lane // EDGE == at
        head = jnp.where(here, pltpu.roll(own_ref[at], at * EDGE, 1), head)
        tail = jnp.where(here, pltpu.roll(own_ref[at], (at + 1) * EDGE, 1), tail)
    head_ref[...] = head
    tail_ref[...] = tail
    store.wait()


def others_kernel(
    start, live_ref, picked_hbm, weights_hbm, cells_hbm, old_hbm,
    flux_hbm, done_ref,
    picked_ref, weights_ref, cells_ref, part_ref, spread_ref, total_ref, sems,
):
    groups = picked_ref.shape[0]
    first, loads = load_blocks(picked_hbm, cells_hbm, weights_hbm, picked_ref, cells_ref, weights_ref, sems)
    for copy in first:
        copy.wait()
    accumulate(slice(start, start + FORCED), live_ref, picked_ref, weights_ref, cells_ref, spread_ref, total_ref, loads)
    lay_out(total_ref, part_ref)
    store = pltpu.make_async_copy(part_ref, flux_hbm.at[pl.ds(start, FORCED)], sems.at[2 + groups])
    store.start()
    done_ref[0] = start
    store.wait()


def block_scratch(picked, weights, cells):
    return [
        pltpu.VMEM(picked.shape, BF16),
        pltpu.VMEM(weights.shape[2:], BF16),
        pltpu.VMEM(cells.shape, jnp.int32),
    ]


def sum_scratch(count, width, rows, cols):
    return [
        pltpu.VMEM((count, rows, cols), F32),
        pltpu.VMEM((HIGH * 2 * count, width), BF16),
        pltpu.VMEM((HIGH * 2 * count, rows // HIGH * cols), F32),
    ]


def remap_forced(live, picked, weights, cells, depth, wet, level, east, north):
    groups, nfield, width = picked.shape
    rows, cols = depth.shape
    tile = jax.ShapeDtypeStruct((rows, cols), F32)
    return pl.pallas_call(
        forced_kernel,
        in_specs=[SMEM] + [HBM] * 8,
        out_specs=[HBM] + [VMEM] * 3,
        out_shape=[
            jax.ShapeDtypeStruct((nfield, rows, cols), F32),
            jax.ShapeDtypeStruct((KEPT, rows, cols), F32),
            tile,
            tile,
        ],
        scratch_shapes=[
            *block_scratch(picked, weights, cells),
            pltpu.VMEM((rows, cols), jnp.int32),
            *sum_scratch(FORCED, width, rows, cols),
            pltpu.SemaphoreType.DMA((groups + 8,)),
        ],
        compiler_params=params(56),
    )(live, picked, weights, cells, depth, wet, level, east, north)


def remap_others(start, live, picked, weights, cells, fluxes):
    groups, _, width = picked.shape
    return pl.pallas_call(
        functools.partial(others_kernel, start),
        in_specs=[SMEM] + [HBM] * 4,
        out_specs=[HBM, SMEM],
        out_shape=[jax.ShapeDtypeStruct(fluxes.shape, F32), jax.ShapeDtypeStruct((1,), jnp.int32)],
        input_output_aliases={4: 0},
        scratch_shapes=[
            *block_scratch(picked, weights, cells),
            *sum_scratch(FORCED, width, *fluxes.shape[1:]),
            pltpu.SemaphoreType.DMA((groups + 3,)),
        ],
        cost_estimate=pl.CostEstimate(flops=2_000_000_000, bytes_accessed=8_000_000, transcendentals=0),
        compiler_params=params(56),
    )(live, picked, weights, cells, fluxes)


def relay_kernel(after_ref, in_ref, out_ref):
    out_ref[...] = in_ref[...]


def edges_kernel(own_ref, east_ref, west_ref, top_ref, bottom_ref):
    rows = own_ref.shape[1]
    for ref, part in ((top_ref, slice(0, EDGE)), (bottom_ref, slice(rows - EDGE, rows))):
        ref[:KEPT] = own_ref[:, part, :]
        ref[KEPT] = east_ref[part, :]
        ref[KEPT + 1] = west_ref[part, :]


def beside(at, east, west):
    lane = lax.broadcasted_iota(jnp.int32, east.shape, 1)
    return jnp.where(
        lane < 64,
        pltpu.roll(east, (128 - at * EDGE) % 128, 1),
        pltpu.roll(west, (128 - EDGE - at * EDGE) % 128, 1),
    )


def extended(at, own_ref, east_ref, west_ref, after_ref, before_ref):
    left = jnp.concatenate([own_ref[at], after_ref[at], before_ref[at]], axis=0)
    right = [beside(at, east_ref[...], west_ref[...])]
    right += [beside(at, ref[KEPT], ref[KEPT + 1]) for ref in (after_ref, before_ref)]
    return jnp.concatenate([left, jnp.concatenate(right, axis=0)], axis=1)


def turning(first_row, total_rows, shape):
    row = lax.broadcasted_iota(jnp.int32, shape, 0)
    row = first_row + jnp.where(row < shape[0] - EDGE, row, row - shape[0])
    return 0.1 + 0.4 * (row.astype(F32) + 0.5) / total_rows


def subcycle(first_row, total_rows, depth, wet, level, east, north, push_x, push_y, fresh, peak):
    step_dt = courant / peak
    rotation = turning(first_row, total_rows, depth.shape)
    flux_x = depth * east * wet
    flux_y = depth * north * wet
    diverge = 0.5 * (across(flux_x) + along(flux_y))
    level = wet * (level + step_dt * (fresh - diverge))
    grad_x = 0.5 * across(level)
    grad_y = 0.5 * along(level)
    new_east = wet * (east + step_dt * (rotation * north - grad_x + push_x - friction * east))
    new_north = wet * (north + step_dt * (-rotation * east - grad_y + push_y - friction * north))
    return level, new_east, new_north


def across(x):
    return pltpu.roll(x, x.shape[1] - 1, 1) - pltpu.roll(x, 1, 1)


def along(x):
    return pltpu.roll(x, x.shape[0] - 1, 0) - pltpu.roll(x, 1, 0)


SAMPLES = ((0.5, 0.0), (0.25, 0.0), (0.5, 0.25), (0.25, 0.12))
SLOT = 32
TERMS = 19
CLOSE = 4e-6


def curve(terms, p, q):
    def one(c):
        parts = [c[3 * a] + q * (c[3 * a + 1] + q * c[3 * a + 2]) for a in range(3)]
        return jnp.abs(parts[0] + p * (parts[1] + p * parts[2]))

    return terms[0] + one(terms[1:10]) + one(terms[10:19])


def powers(depth, wet, rotation, level, east, north, push_x=None, push_y=None, fresh=None):
    drift = -0.5 * (across(depth * east * wet) + along(depth * north * wet))
    turn_x, turn_y = rotation * north - friction * east, -rotation * east - friction * north
    if fresh is not None:
        drift, turn_x, turn_y = drift + fresh, turn_x + push_x, turn_y + push_y
    drift = wet * drift
    if level is not None:
        still = wet * level
        turn_x, turn_y = turn_x - 0.5 * across(still), turn_y - 0.5 * along(still)
    else:
        still = None
    return (
        (still, wet * east, wet * north),
        (drift, wet * turn_x, wet * turn_y),
        (None, wet * (-0.5 * across(drift)), wet * (-0.5 * along(drift))),
    )


def offers(rotation, depth, wet, level, east, north, push_x, push_y, fresh):
    own = (slice(0, depth.shape[0] - 2 * EDGE), slice(0, 128))
    forcing = (push_x, push_y, fresh)
    u, v = [], []
    for a, part in enumerate(powers(depth, wet, rotation, level, east, north, *forcing)):
        for two in powers(depth, wet, rotation, *part, *(forcing if a == 0 else ())):
            u.append(two[1][own])
            v.append(two[2][own])
    terms = [jnp.sqrt(depth[own])] + u + v
    shape = terms[0].shape
    index = lax.broadcasted_iota(jnp.int32, shape, 0) * 128 + lax.broadcasted_iota(jnp.int32, shape, 1)
    lane = lax.broadcasted_iota(jnp.int32, (1, 128), 1)
    peak = peak_of(depth[own], wet[own], east[own], north[own])
    dt = courant / peak
    row = jnp.where(lane == SLOT - 1, peak, 0.0)
    for j, (p, q) in enumerate(SAMPLES):
        speed = curve(terms, p * dt, q * dt)
        fastest = speed == jnp.max(speed, keepdims=True)
        first = jnp.min(jnp.where(fastest, index, shape[0] * 128), keepdims=True)
        for i, term in enumerate(terms):
            value = jnp.sum(jnp.where(index == first, term, 0.0), keepdims=True)
            row = jnp.where(lane == SLOT * j + i, value, row)
    return row


def offered(rows, p, q):
    lane = lax.broadcasted_iota(jnp.int32, rows.shape, 1)
    terms = [rows] + [pltpu.roll(rows, 128 - i, 1) for i in range(1, TERMS)]
    return jnp.where(lane % SLOT == 0, curve(terms, p, q), 0.0)


def choose_kernel(rows_ref, out_ref):
    rows = rows_ref[...]
    count = rows.shape[0]
    lane = lax.broadcasted_iota(jnp.int32, rows.shape, 1)
    dt = courant / lane_max(rows, SLOT - 1)
    p, q = jnp.zeros(rows.shape, F32), jnp.zeros(rows.shape, F32)
    for j, (first, second) in enumerate(SAMPLES):
        p = jnp.where(lane // SLOT == j, first, p)
        q = jnp.where(lane // SLOT == j, second, q)
    speed = offered(rows, p * dt, q * dt)
    number = lax.broadcasted_iota(jnp.int32, rows.shape, 0)
    best = jnp.min(jnp.where(speed == jnp.max(speed, axis=0, keepdims=True), number, count), axis=0, keepdims=True)
    chosen = jnp.where((number == best) & (lane % SLOT == 0), 1.0, 0.0)
    for shift in (1, 2, 4, 8, 16):
        chosen = chosen + pltpu.roll(chosen, shift, 1)
    row = jnp.sum(jnp.where(chosen > 0.0, rows, 0.0), axis=0, keepdims=True)
    row = jnp.where(lane[:1] == SLOT - 1, jnp.max(rows, axis=0, keepdims=True), row)
    out_ref[...] = jnp.broadcast_to(row, out_ref.shape)


def lane_max(rows, at):
    lane = lax.broadcasted_iota(jnp.int32, rows.shape, 1)
    return jnp.max(jnp.where(lane == at, rows, 0.0), keepdims=True)


def offer_kernel(
    total_rows, row_ref, own_ref, east_ref, west_ref, after_ref, before_ref, kept_ref, state_ref, row_out_ref
):
    full = [extended(at, own_ref, east_ref, west_ref, after_ref, before_ref) for at in range(KEPT)]
    depth, wet, level, east, north, push_x, push_y, fresh = full
    for at, array in enumerate((depth, wet, push_x, push_y, fresh)):
        kept_ref[at] = array
    for at, array in enumerate((level, east, north)):
        state_ref[at] = array
    rotation = turning(row_ref[0], total_rows, depth.shape)
    row = offers(rotation, depth, wet, level, east, north, push_x, push_y, fresh)
    row_out_ref[...] = jnp.broadcast_to(row, row_out_ref.shape)


def most_kernel(rows_ref, out_ref):
    out_ref[...] = jnp.broadcast_to(jnp.max(rows_ref[...], axis=0, keepdims=True), out_ref.shape)


def everyone(peak):
    row = jax.ShapeDtypeStruct((axes_size(COLUMN), 128), F32)
    return exchange(call_small(most_kernel, (), (exchange(peak, PLANE),), row), COLUMN)


def step_from(total_rows, row_ref, kept_ref, old, peak):
    return subcycle(
        row_ref[0], total_rows, kept_ref[0], kept_ref[1], *old, kept_ref[2], kept_ref[3], kept_ref[4], peak
    )


def local_peak(kept_ref, state):
    depth, wet = kept_ref[0], kept_ref[1]
    own = (slice(0, depth.shape[0] - 2 * EDGE), slice(0, 128))
    return peak_of(depth[own], wet[own], state[1][own], state[2][own])


def middle_kernel(total_rows, row_ref, kept_ref, old_ref, rows_ref, third_ref, peak_ref, guess_ref):
    rows = rows_ref[...]
    peaks = [lane_max(rows, SLOT - 1)]
    peaks.append(jnp.max(offered(rows, courant / peaks[0], 0.0), keepdims=True))
    peaks.append(jnp.max(offered(rows, courant / peaks[0], courant / peaks[1]), keepdims=True))
    state = [old_ref[at] for at in range(3)]
    lane = lax.broadcasted_iota(jnp.int32, (1, 128), 1)
    row = jnp.zeros((1, 128), F32)
    for at in range(3):
        state = step_from(total_rows, row_ref, kept_ref, state, peaks[at])
        row = jnp.where(lane == at, local_peak(kept_ref, state), row)
    for at in range(3):
        third_ref[at] = state[at]
    peak_ref[...] = jnp.broadcast_to(row, peak_ref.shape)
    guess_ref[...] = jnp.broadcast_to(jnp.where(lane == 0, peaks[1], peaks[2]), guess_ref.shape)


def last_kernel(total_rows, row_ref, kept_ref, old_ref, rows_ref, guess_ref, out_ref, good_ref):
    rows = rows_ref[...]
    new = step_from(total_rows, row_ref, kept_ref, [old_ref[at] for at in range(3)], lane_max(rows, 2))
    for at in range(3):
        out_ref[at] = new[at][: out_ref.shape[1], :128]
    lane = lax.broadcasted_iota(jnp.int32, (1, 128), 1)
    true = jnp.max(rows, axis=0, keepdims=True)
    off = jnp.where(lane < 2, jnp.abs(true - guess_ref[0:1, :]) - CLOSE * true, -1.0)
    good_ref[0] = jnp.where(jnp.max(off) <= 0.0, 1, 0)


def redo_kernel(total_rows, at, row_ref, kept_ref, old_ref, rows_ref, state_ref, peak_ref):
    new = step_from(total_rows, row_ref, kept_ref, [old_ref[i] for i in range(3)], lane_max(rows_ref[...], at))
    for i in range(3):
        state_ref[i] = new[i]
    peak_ref[...] = jnp.broadcast_to(local_peak(kept_ref, new), peak_ref.shape)


def call_small(kernel, scalars, arrays, out_shape, out_specs=None):
    return pl.pallas_call(
        kernel,
        in_specs=[SMEM] * len(scalars) + [VMEM] * len(arrays),
        out_shape=out_shape,
        out_specs=jax.tree.map(lambda _: VMEM, out_shape) if out_specs is None else out_specs,
        compiler_params=params(8),
    )(*scalars, *arrays)


def shards(
    atm_fields,
    send_cols,
    live_blocks,
    remap_weights,
    row_map,
    ocean_depth,
    wet_mask,
    sea_level,
    east_vel,
    north_vel,
):
    rows, cols = ocean_depth.shape
    total_rows = rows * axes_size(DOM)
    first_row = (lax.axis_index(DOM) * rows).reshape(1).astype(jnp.int32)
    wide = (rows + 2 * EDGE, 2 * cols)
    three = jax.ShapeDtypeStruct((3, *wide), F32)
    five = jax.ShapeDtypeStruct((5, *wide), F32)
    rim = jax.ShapeDtypeStruct((KEPT + 2, EDGE, cols), F32)
    peak_shape = jax.ShapeDtypeStruct((axes_size(PLANE), 128), F32)

    picked = pick(atm_fields, send_cols)
    received = lax.all_to_all(picked, "comp", split_axis=0, concat_axis=0, tiled=True)
    fluxes, own, head, tail = remap_forced(
        live_blocks, received, remap_weights, row_map, ocean_depth, wet_mask, sea_level, east_vel, north_vel
    )
    east, west = neighbours(head, tail, ("comp",))
    blocks = (live_blocks, received, remap_weights, row_map)
    fluxes, done = remap_others(FORCED, *blocks, fluxes)
    own = call_small(relay_kernel, (done,), (own,), jax.ShapeDtypeStruct(own.shape, F32))
    top, bottom = call_small(edges_kernel, (), (own, east, west), [rim, rim])
    after, before = neighbours(top, bottom, DOM)
    fluxes, _ = remap_others(2 * FORCED, *blocks, fluxes)
    kept, start, row = call_small(
        functools.partial(offer_kernel, total_rows),
        (first_row,),
        (own, east, west, after, before),
        [five, three, peak_shape],
    )
    (row,) = call_small(
        choose_kernel, (), (exchange(row, PLANE),), [jax.ShapeDtypeStruct((axes_size(COLUMN), 128), F32)]
    )
    first = exchange(row, COLUMN)
    third, peak, guess = call_small(
        functools.partial(middle_kernel, total_rows),
        (first_row,),
        (kept, start, first),
        [three, peak_shape, jax.ShapeDtypeStruct((8, 128), F32)],
    )

    def last(third, seen):
        return call_small(
            functools.partial(last_kernel, total_rows),
            (first_row,),
            (kept, third, seen, guess),
            [jax.ShapeDtypeStruct((3, rows, cols), F32), jax.ShapeDtypeStruct((1,), jnp.int32)],
            [VMEM, SMEM],
        )

    state, good = last(third, everyone(peak))

    def again():
        state, seen, at = start, first, SLOT - 1
        for _ in range(3):
            state, peak = call_small(
                functools.partial(redo_kernel, total_rows, at), (first_row,), (kept, state, seen), [three, peak_shape]
            )
            seen, at = everyone(peak), 2
        return last(state, seen)[0]

    state = lax.cond(good[0] == 1, lambda: state, again)
    return fluxes, state


def solution(mesh):
    split = Mesh(mesh.devices.reshape(mesh.shape["comp"], *DOM_SHAPE), COMP_DOM)
    return jax.shard_map(
        shards,
        mesh=split,
        in_specs=(
            P(None, COMP_DOM),
            P("comp", DOM, None, None, None),
            P("comp", DOM, None),
            P("comp", DOM, None, None, None, None),
            P("comp", DOM, None, None, None),
            P(DOM, "comp"),
            P(DOM, "comp"),
            P(DOM, "comp"),
            P(DOM, "comp"),
            P(DOM, "comp"),
        ),
        out_specs=(P(None, DOM, "comp"), P(None, DOM, "comp")),
        check_vma=False,
    )
```

```python
import functools

import jax
import jax.numpy as jnp
from jax import lax
from jax.experimental import pallas as pl
from jax.experimental.pallas import tpu as pltpu
from jax.sharding import Mesh
from jax.sharding import PartitionSpec as P

DOM_SHAPE = (12, 4, 2)
COMP_DOM = ("comp", "dom_0", "dom_1", "dom_2")
DOM = ("dom_0", "dom_1", "dom_2")
PLANE = ("comp", "dom_1")
COLUMN = ("dom_0", "dom_2")
BF16 = jnp.bfloat16
F32 = jnp.float32

courant = 0.5
friction = 0.05

EDGE = 8
KEPT = 8
HIGH = 8
NT = (((1,), (1,)), ((), ()))
HBM = pl.BlockSpec(memory_space=pltpu.HBM)
SMEM = pl.BlockSpec(memory_space=pltpu.SMEM)
VMEM = pl.BlockSpec(memory_space=pltpu.VMEM)


def params(mib):
    return pltpu.CompilerParams(vmem_limit_bytes=mib * 1024 * 1024)


def axes_size(axes):
    return functools.reduce(lambda a, b: a * b, [lax.axis_size(a) for a in axes])


def neighbours(head, tail, axes):
    count = axes_size(axes)
    after = lax.ppermute(head, axes, [(i + 1, i) for i in range(count - 1)])
    before = lax.ppermute(tail, axes, [(i, i + 1) for i in range(count - 1)])
    return after, before


def fetch(refs, buffers, sems, first=0):
    copies = [pltpu.make_async_copy(ref, buf, sems.at[first + i]) for i, (ref, buf) in enumerate(zip(refs, buffers))]
    for copy in copies:
        copy.start()
    return copies


def rows16(row, count):
    tile = jnp.broadcast_to(row.astype(F32), (16, row.shape[1])).astype(BF16)
    return jnp.concatenate([tile] * (count // 16), axis=0)


def onehot(row, count):
    at = lax.broadcasted_iota(jnp.int32, (count, row.shape[1]), 0).astype(F32).astype(BF16)
    return jnp.where(at == rows16(row, count), jnp.ones_like(at), jnp.zeros_like(at))


def pick_kernel(fields_hbm, cols_hbm, out_ref, fields_ref, cols_ref, sems):
    for copy in fetch((fields_hbm, cols_hbm), (fields_ref, cols_ref), sems):
        copy.wait()
    nfield, ncol = fields_ref.shape
    high = ncol // 256
    rows = [fields_ref[:, h * 256 : (h + 1) * 256].astype(F32) for h in range(high)]
    table = jnp.concatenate(rows, axis=0).astype(BF16)
    groups, blocks, width = cols_ref.shape[2:]
    for c in range(groups):
        for k in range(blocks):
            cols = cols_ref[0, 0, c, k : k + 1, :]
            both = jnp.dot(table, onehot(cols & 255, 256), preferred_element_type=F32)
            upper = jnp.broadcast_to(cols >> 8, (nfield, width))
            picked = both[:nfield]
            for h in range(1, high):
                picked = jnp.where(upper == h, both[h * nfield : (h + 1) * nfield], picked)
            out_ref[c, :, k * width : (k + 1) * width] = picked.astype(BF16)


def pick(fields, cols):
    groups, blocks, width = cols.shape[2:]
    return pl.pallas_call(
        pick_kernel,
        in_specs=[HBM] * 2,
        out_specs=VMEM,
        out_shape=jax.ShapeDtypeStruct((groups, fields.shape[0], blocks * width), BF16),
        scratch_shapes=[
            pltpu.VMEM(fields.shape, BF16),
            pltpu.VMEM(cols.shape, jnp.int32),
            pltpu.SemaphoreType.DMA((2,)),
        ],
        compiler_params=params(56),
    )(fields, cols)


def peak_of(depth, wet, east, north):
    return jnp.max(jnp.sqrt(depth) + wet * (jnp.abs(east) + jnp.abs(north)), keepdims=True)


def exchange(peak, axes):
    return lax.all_to_all(peak, axes, split_axis=0, concat_axis=0, tiled=True)


def remap_kernel(
    live_ref, picked_hbm, weights_hbm, cells_hbm, depth_hbm, wet_hbm, level_hbm, east_hbm, north_hbm,
    flux_ref, own_ref, head_ref, tail_ref,
    picked_ref, weights_ref, cells_ref, wet_ref, spread_ref, total_ref, sems,
):
    groups, nfield, width = picked_ref.shape
    blocks = weights_ref.shape[1]
    pair_rows = 2 * nfield
    lows = total_ref.shape[1]
    first = fetch((picked_hbm, cells_hbm), (picked_ref, cells_ref), sems)
    loads = fetch([weights_hbm.at[0, 0, c] for c in range(groups)], [weights_ref.at[c] for c in range(groups)], sems, 2)
    rest = fetch(
        (depth_hbm, level_hbm, east_hbm, north_hbm, wet_hbm),
        (own_ref.at[0], own_ref.at[2], own_ref.at[3], own_ref.at[4], wet_ref),
        sems,
        2 + groups,
    )
    for copy in first:
        copy.wait()
    for c in range(groups):
        loads[c].wait()
        live = live_ref[0, 0, c]
        onehots = []
        for k in range(blocks):
            part = slice(k * 256, (k + 1) * 256)
            contrib = lax.dot_general(picked_ref[c, :, part], weights_ref[c, k], NT, preferred_element_type=F32)
            big = contrib.astype(BF16).astype(F32)
            pair = jnp.concatenate([big, contrib - big], axis=0).astype(BF16)
            cell = cells_ref[0, 0, c, k : k + 1, :]
            upper = rows16(jnp.where(jnp.int32(k) < live, (cell >> 7) & (HIGH - 1), -1), pair_rows)
            for h in range(HIGH):
                spread_ref[h * pair_rows : (h + 1) * pair_rows, part] = jnp.where(
                    upper == BF16(h), pair, jnp.zeros_like(pair)
                )
            row, column = cell >> 7, cell & 127
            low = (row // HIGH) * 128 + column
            tiles = [onehot(jnp.where(low >> 8 == t, low & 255, -1), 256) for t in range(lows // 256)]
            onehots.append(jnp.concatenate(tiles, axis=0))
        added = lax.dot_general(
            spread_ref[...], jnp.concatenate(onehots, axis=1), NT, preferred_element_type=F32
        )
        if c == 0:
            total_ref[...] = added
        else:
            total_ref[...] += added
    for h in range(HIGH):
        base = h * pair_rows
        both = total_ref[base : base + nfield, :] + total_ref[base + nfield : base + pair_rows, :]
        for r in range(lows // 128):
            flux_ref[:, r * HIGH + h, :] = both[:, r * 128 : (r + 1) * 128]
    for copy in rest:
        copy.wait()
    own_ref[1] = wet_ref[...].astype(F32)
    own_ref[5] = flux_ref[0] / own_ref[0]
    own_ref[6] = flux_ref[1] / own_ref[0]
    own_ref[7] = flux_ref[2]
    lane = lax.broadcasted_iota(jnp.int32, head_ref.shape, 1)
    head = own_ref[0]
    tail = pltpu.roll(own_ref[0], EDGE, 1)
    for at in range(1, KEPT):
        here = lane // EDGE == at
        head = jnp.where(here, pltpu.roll(own_ref[at], at * EDGE, 1), head)
        tail = jnp.where(here, pltpu.roll(own_ref[at], (at + 1) * EDGE, 1), tail)
    head_ref[...] = head
    tail_ref[...] = tail


def remap(live, picked, weights, cells, depth, wet, level, east, north):
    groups, nfield, width = picked.shape
    rows, cols = depth.shape
    tile = jax.ShapeDtypeStruct((rows, cols), F32)
    return pl.pallas_call(
        remap_kernel,
        in_specs=[SMEM] + [HBM] * 8,
        out_specs=[VMEM] * 4,
        out_shape=[
            jax.ShapeDtypeStruct((nfield, rows, cols), F32),
            jax.ShapeDtypeStruct((KEPT, rows, cols), F32),
            tile,
            tile,
        ],
        scratch_shapes=[
            pltpu.VMEM(picked.shape, BF16),
            pltpu.VMEM(weights.shape[2:], BF16),
            pltpu.VMEM(cells.shape, jnp.int32),
            pltpu.VMEM((rows, cols), jnp.int32),
            pltpu.VMEM((HIGH * 2 * nfield, cells.shape[3] * cells.shape[4]), BF16),
            pltpu.VMEM((HIGH * 2 * nfield, rows // HIGH * cols), F32),
            pltpu.SemaphoreType.DMA((groups + 7,)),
        ],
        compiler_params=params(56),
    )(live, picked, weights, cells, depth, wet, level, east, north)


def relay_kernel(in_ref, out_ref):
    out_ref[...] = in_ref[...]


def edges_kernel(own_ref, east_ref, west_ref, top_ref, bottom_ref):
    rows = own_ref.shape[1]
    for ref, part in ((top_ref, slice(0, EDGE)), (bottom_ref, slice(rows - EDGE, rows))):
        ref[:KEPT] = own_ref[:, part, :]
        ref[KEPT] = east_ref[part, :]
        ref[KEPT + 1] = west_ref[part, :]


def beside(at, east, west):
    lane = lax.broadcasted_iota(jnp.int32, east.shape, 1)
    return jnp.where(
        lane < 64,
        pltpu.roll(east, (128 - at * EDGE) % 128, 1),
        pltpu.roll(west, (128 - EDGE - at * EDGE) % 128, 1),
    )


def extended(at, own_ref, east_ref, west_ref, after_ref, before_ref):
    left = jnp.concatenate([own_ref[at], after_ref[at], before_ref[at]], axis=0)
    right = [beside(at, east_ref[...], west_ref[...])]
    right += [beside(at, ref[KEPT], ref[KEPT + 1]) for ref in (after_ref, before_ref)]
    return jnp.concatenate([left, jnp.concatenate(right, axis=0)], axis=1)


def turning(first_row, total_rows, shape):
    row = lax.broadcasted_iota(jnp.int32, shape, 0)
    row = first_row + jnp.where(row < shape[0] - EDGE, row, row - shape[0])
    return 0.1 + 0.4 * (row.astype(F32) + 0.5) / total_rows


def subcycle(first_row, total_rows, depth, wet, level, east, north, push_x, push_y, fresh, peak):
    step_dt = courant / peak
    rotation = turning(first_row, total_rows, depth.shape)
    flux_x = depth * east * wet
    flux_y = depth * north * wet
    diverge = 0.5 * (across(flux_x) + along(flux_y))
    level = wet * (level + step_dt * (fresh - diverge))
    grad_x = 0.5 * across(level)
    grad_y = 0.5 * along(level)
    new_east = wet * (east + step_dt * (rotation * north - grad_x + push_x - friction * east))
    new_north = wet * (north + step_dt * (-rotation * east - grad_y + push_y - friction * north))
    return level, new_east, new_north


def across(x):
    return pltpu.roll(x, x.shape[1] - 1, 1) - pltpu.roll(x, 1, 1)


def along(x):
    return pltpu.roll(x, x.shape[0] - 1, 0) - pltpu.roll(x, 1, 0)


SAMPLES = ((0.5, 0.0), (0.25, 0.0), (0.5, 0.25), (0.25, 0.12))
SLOT = 32
TERMS = 19
CLOSE = 4e-6


def curve(terms, p, q):
    def one(c):
        parts = [c[3 * a] + q * (c[3 * a + 1] + q * c[3 * a + 2]) for a in range(3)]
        return jnp.abs(parts[0] + p * (parts[1] + p * parts[2]))

    return terms[0] + one(terms[1:10]) + one(terms[10:19])


def powers(depth, wet, rotation, level, east, north, push_x=None, push_y=None, fresh=None):
    drift = -0.5 * (across(depth * east * wet) + along(depth * north * wet))
    turn_x, turn_y = rotation * north - friction * east, -rotation * east - friction * north
    if fresh is not None:
        drift, turn_x, turn_y = drift + fresh, turn_x + push_x, turn_y + push_y
    drift = wet * drift
    if level is not None:
        still = wet * level
        turn_x, turn_y = turn_x - 0.5 * across(still), turn_y - 0.5 * along(still)
    else:
        still = None
    return (
        (still, wet * east, wet * north),
        (drift, wet * turn_x, wet * turn_y),
        (None, wet * (-0.5 * across(drift)), wet * (-0.5 * along(drift))),
    )


def offers(rotation, depth, wet, level, east, north, push_x, push_y, fresh):
    own = (slice(0, depth.shape[0] - 2 * EDGE), slice(0, 128))
    forcing = (push_x, push_y, fresh)
    u, v = [], []
    for a, part in enumerate(powers(depth, wet, rotation, level, east, north, *forcing)):
        for two in powers(depth, wet, rotation, *part, *(forcing if a == 0 else ())):
            u.append(two[1][own])
            v.append(two[2][own])
    terms = [jnp.sqrt(depth[own])] + u + v
    shape = terms[0].shape
    index = lax.broadcasted_iota(jnp.int32, shape, 0) * 128 + lax.broadcasted_iota(jnp.int32, shape, 1)
    lane = lax.broadcasted_iota(jnp.int32, (1, 128), 1)
    peak = peak_of(depth[own], wet[own], east[own], north[own])
    dt = courant / peak
    row = jnp.where(lane == SLOT - 1, peak, 0.0)
    for j, (p, q) in enumerate(SAMPLES):
        speed = curve(terms, p * dt, q * dt)
        fastest = speed == jnp.max(speed, keepdims=True)
        first = jnp.min(jnp.where(fastest, index, shape[0] * 128), keepdims=True)
        for i, term in enumerate(terms):
            value = jnp.sum(jnp.where(index == first, term, 0.0), keepdims=True)
            row = jnp.where(lane == SLOT * j + i, value, row)
    return row


def offered(rows, p, q):
    lane = lax.broadcasted_iota(jnp.int32, rows.shape, 1)
    terms = [rows] + [pltpu.roll(rows, 128 - i, 1) for i in range(1, TERMS)]
    return jnp.where(lane % SLOT == 0, curve(terms, p, q), 0.0)


def choose_kernel(rows_ref, out_ref):
    rows = rows_ref[...]
    count = rows.shape[0]
    lane = lax.broadcasted_iota(jnp.int32, rows.shape, 1)
    dt = courant / lane_max(rows, SLOT - 1)
    p, q = jnp.zeros(rows.shape, F32), jnp.zeros(rows.shape, F32)
    for j, (first, second) in enumerate(SAMPLES):
        p = jnp.where(lane // SLOT == j, first, p)
        q = jnp.where(lane // SLOT == j, second, q)
    speed = offered(rows, p * dt, q * dt)
    number = lax.broadcasted_iota(jnp.int32, rows.shape, 0)
    best = jnp.min(jnp.where(speed == jnp.max(speed, axis=0, keepdims=True), number, count), axis=0, keepdims=True)
    chosen = jnp.where((number == best) & (lane % SLOT == 0), 1.0, 0.0)
    for shift in (1, 2, 4, 8, 16):
        chosen = chosen + pltpu.roll(chosen, shift, 1)
    row = jnp.sum(jnp.where(chosen > 0.0, rows, 0.0), axis=0, keepdims=True)
    row = jnp.where(lane[:1] == SLOT - 1, jnp.max(rows, axis=0, keepdims=True), row)
    out_ref[...] = jnp.broadcast_to(row, out_ref.shape)


def lane_max(rows, at):
    lane = lax.broadcasted_iota(jnp.int32, rows.shape, 1)
    return jnp.max(jnp.where(lane == at, rows, 0.0), keepdims=True)


def offer_kernel(
    total_rows, row_ref, own_ref, east_ref, west_ref, after_ref, before_ref, kept_ref, state_ref, row_out_ref
):
    full = [extended(at, own_ref, east_ref, west_ref, after_ref, before_ref) for at in range(KEPT)]
    depth, wet, level, east, north, push_x, push_y, fresh = full
    for at, array in enumerate((depth, wet, push_x, push_y, fresh)):
        kept_ref[at] = array
    for at, array in enumerate((level, east, north)):
        state_ref[at] = array
    rotation = turning(row_ref[0], total_rows, depth.shape)
    row = offers(rotation, depth, wet, level, east, north, push_x, push_y, fresh)
    row_out_ref[...] = jnp.broadcast_to(row, row_out_ref.shape)


def most_kernel(rows_ref, out_ref):
    out_ref[...] = jnp.broadcast_to(jnp.max(rows_ref[...], axis=0, keepdims=True), out_ref.shape)


def everyone(peak):
    row = jax.ShapeDtypeStruct((axes_size(COLUMN), 128), F32)
    return exchange(call_small(most_kernel, (), (exchange(peak, PLANE),), row), COLUMN)


def step_from(total_rows, row_ref, kept_ref, old, peak):
    return subcycle(
        row_ref[0], total_rows, kept_ref[0], kept_ref[1], *old, kept_ref[2], kept_ref[3], kept_ref[4], peak
    )


def local_peak(kept_ref, state):
    depth, wet = kept_ref[0], kept_ref[1]
    own = (slice(0, depth.shape[0] - 2 * EDGE), slice(0, 128))
    return peak_of(depth[own], wet[own], state[1][own], state[2][own])


def middle_kernel(total_rows, row_ref, kept_ref, old_ref, rows_ref, third_ref, peak_ref, guess_ref):
    rows = rows_ref[...]
    peaks = [lane_max(rows, SLOT - 1)]
    peaks.append(jnp.max(offered(rows, courant / peaks[0], 0.0), keepdims=True))
    peaks.append(jnp.max(offered(rows, courant / peaks[0], courant / peaks[1]), keepdims=True))
    state = [old_ref[at] for at in range(3)]
    lane = lax.broadcasted_iota(jnp.int32, (1, 128), 1)
    row = jnp.zeros((1, 128), F32)
    for at in range(3):
        state = step_from(total_rows, row_ref, kept_ref, state, peaks[at])
        row = jnp.where(lane == at, local_peak(kept_ref, state), row)
    for at in range(3):
        third_ref[at] = state[at]
    peak_ref[...] = jnp.broadcast_to(row, peak_ref.shape)
    guess_ref[...] = jnp.broadcast_to(jnp.where(lane == 0, peaks[1], peaks[2]), guess_ref.shape)


def last_kernel(total_rows, row_ref, kept_ref, old_ref, rows_ref, guess_ref, out_ref, good_ref):
    rows = rows_ref[...]
    new = step_from(total_rows, row_ref, kept_ref, [old_ref[at] for at in range(3)], lane_max(rows, 2))
    for at in range(3):
        out_ref[at] = new[at][: out_ref.shape[1], :128]
    lane = lax.broadcasted_iota(jnp.int32, (1, 128), 1)
    true = jnp.max(rows, axis=0, keepdims=True)
    off = jnp.where(lane < 2, jnp.abs(true - guess_ref[0:1, :]) - CLOSE * true, -1.0)
    good_ref[0] = jnp.where(jnp.max(off) <= 0.0, 1, 0)


def redo_kernel(total_rows, at, row_ref, kept_ref, old_ref, rows_ref, state_ref, peak_ref):
    new = step_from(total_rows, row_ref, kept_ref, [old_ref[i] for i in range(3)], lane_max(rows_ref[...], at))
    for i in range(3):
        state_ref[i] = new[i]
    peak_ref[...] = jnp.broadcast_to(local_peak(kept_ref, new), peak_ref.shape)


def call_small(kernel, scalars, arrays, out_shape, out_specs=None):
    return pl.pallas_call(
        kernel,
        in_specs=[SMEM] * len(scalars) + [VMEM] * len(arrays),
        out_shape=out_shape,
        out_specs=jax.tree.map(lambda _: VMEM, out_shape) if out_specs is None else out_specs,
        compiler_params=params(8),
    )(*scalars, *arrays)


def shards(
    atm_fields,
    send_cols,
    live_blocks,
    remap_weights,
    row_map,
    ocean_depth,
    wet_mask,
    sea_level,
    east_vel,
    north_vel,
):
    rows, cols = ocean_depth.shape
    total_rows = rows * axes_size(DOM)
    first_row = (lax.axis_index(DOM) * rows).reshape(1).astype(jnp.int32)
    wide = (rows + 2 * EDGE, 2 * cols)
    three = jax.ShapeDtypeStruct((3, *wide), F32)
    five = jax.ShapeDtypeStruct((5, *wide), F32)
    rim = jax.ShapeDtypeStruct((KEPT + 2, EDGE, cols), F32)
    peak_shape = jax.ShapeDtypeStruct((axes_size(PLANE), 128), F32)

    picked = pick(atm_fields, send_cols)
    received = lax.all_to_all(picked, "comp", split_axis=0, concat_axis=0, tiled=True)
    fluxes, own, head, tail = remap(
        live_blocks, received, remap_weights, row_map, ocean_depth, wet_mask, sea_level, east_vel, north_vel
    )
    east, west = neighbours(head, tail, ("comp",))
    own = call_small(relay_kernel, (), (own,), jax.ShapeDtypeStruct(own.shape, F32))
    top, bottom = call_small(edges_kernel, (), (own, east, west), [rim, rim])
    after, before = neighbours(top, bottom, DOM)
    kept, start, row = call_small(
        functools.partial(offer_kernel, total_rows),
        (first_row,),
        (own, east, west, after, before),
        [five, three, peak_shape],
    )
    (row,) = call_small(
        choose_kernel, (), (exchange(row, PLANE),), [jax.ShapeDtypeStruct((axes_size(COLUMN), 128), F32)]
    )
    first = exchange(row, COLUMN)
    third, peak, guess = call_small(
        functools.partial(middle_kernel, total_rows),
        (first_row,),
        (kept, start, first),
        [three, peak_shape, jax.ShapeDtypeStruct((8, 128), F32)],
    )

    def last(third, seen):
        return call_small(
            functools.partial(last_kernel, total_rows),
            (first_row,),
            (kept, third, seen, guess),
            [jax.ShapeDtypeStruct((3, rows, cols), F32), jax.ShapeDtypeStruct((1,), jnp.int32)],
            [VMEM, SMEM],
        )

    state, good = last(third, everyone(peak))

    def again():
        state, seen, at = start, first, SLOT - 1
        for _ in range(3):
            state, peak = call_small(
                functools.partial(redo_kernel, total_rows, at), (first_row,), (kept, state, seen), [three, peak_shape]
            )
            seen, at = everyone(peak), 2
        return last(state, seen)[0]

    state = lax.cond(good[0] == 1, lambda: state, again)
    return fluxes, state


def solution(mesh):
    split = Mesh(mesh.devices.reshape(mesh.shape["comp"], *DOM_SHAPE), COMP_DOM)
    return jax.shard_map(
        shards,
        mesh=split,
        in_specs=(
            P(None, COMP_DOM),
            P("comp", DOM, None, None, None),
            P("comp", DOM, None),
            P("comp", DOM, None, None, None, None),
            P("comp", DOM, None, None, None),
            P(DOM, "comp"),
            P(DOM, "comp"),
            P(DOM, "comp"),
            P(DOM, "comp"),
            P(DOM, "comp"),
        ),
        out_specs=(P(None, DOM, "comp"), P(None, DOM, "comp")),
        check_vma=False,
    )
```
